32 devices in a mesh: rep: 2 (over core), fsdp: 16 (over z, y, x).
Axes of the slice: x: 2, y: 2, z: 4, core: 2. Of those that a mesh axis runs over, the one named last changes fastest.
Arguments:
- hidden_in: bfloat16 [4, 1024, 2048], P('rep', 'fsdp'), may hold values from -6 to 6
- cotangent: bfloat16 [4, 1024, 2048], P('rep', 'fsdp'), may hold values from -6 to 6
- lengths: int32 [4], P('rep'), may hold values from 256 to 1024, as said below
- routes: int32 [4, 1024, 6], P('rep', 'fsdp'), may hold values from 0 to 15, all different within a row; in each aligned block of 64 rows (0 to 63, 64 to 127, ..., all dimensions but the last counted through in order) at most 36 rows name the same one
- gate_values: float32 [4, 1024, 6], P('rep', 'fsdp'), may hold values from 0.25 to 1
- attn_gain: bfloat16 [2048], P('fsdp'), may hold values from 0.5 to 1.5
- query_proj: bfloat16 [2048, 3072], P('fsdp'), may hold values from -0.125 to 0.125
- latent_proj: bfloat16 [2048, 576], P('fsdp'), may hold values from -0.125 to 0.125
- latent_gain: bfloat16 [512], P('fsdp'), may hold values from 0.5 to 1.5
- expand_proj: bfloat16 [512, 4096], P('fsdp'), may hold values from -0.25 to 0.25
- output_proj: bfloat16 [2048, 2048], P('fsdp'), may hold values from -1.5 to 1.5
- ffn_gain: bfloat16 [2048], P('fsdp'), may hold values from 0.5 to 1.5
- shared_gate: bfloat16 [2048, 2816], P('fsdp'), may hold values from -0.125 to 0.125
- shared_lift: bfloat16 [2048, 2816], P('fsdp'), may hold values from -0.125 to 0.125
- shared_down: bfloat16 [2816, 2048], P('fsdp'), may hold values from -0.109375 to 0.109375
- expert_gate: bfloat16 [16, 2048, 1408], P('fsdp', None, 'rep'), may hold values from -0.125 to 0.125
- expert_lift: bfloat16 [16, 2048, 1408], P('fsdp', None, 'rep'), may hold values from -0.125 to 0.125
- expert_down: bfloat16 [16, 1408, 2048], P('fsdp', 'rep'), may hold values from -0.15625 to 0.15625
Outputs:
- block_out: bfloat16 [4, 1024, 2048], P('rep', 'fsdp')
- grad_hidden: bfloat16 [4, 1024, 2048], P('rep', 'fsdp')
- grad_attn_gain: float32 [2048], P('fsdp')
- grad_query_proj: float32 [2048, 3072], P('fsdp')
- grad_latent_proj: float32 [2048, 576], P('fsdp')
- grad_latent_gain: float32 [512], P('fsdp')
- grad_expand_proj: float32 [512, 4096], P('fsdp')
- grad_output_proj: float32 [2048, 2048], P('fsdp')
- grad_ffn_gain: float32 [2048], P('fsdp')
- grad_shared_gate: float32 [2048, 2816], P('fsdp')
- grad_shared_lift: float32 [2048, 2816], P('fsdp')
- grad_shared_down: float32 [2816, 2048], P('fsdp')
- grad_expert_gate: float32 [16, 2048, 1408], P('fsdp', None, 'rep')
- grad_expert_lift: float32 [16, 2048, 1408], P('fsdp', None, 'rep')
- grad_expert_down: float32 [16, 1408, 2048], P('fsdp', 'rep')
The draws below stay inside these ranges and needn't reach their ends.
Inputs may be any that keep to these rules, and one draw needn't show every extreme that they name: `lengths`: in each group of 2 consecutive rows, one row, drawn from the seed, has all 1024 slots used. The 6 routes of a token name different experts. Within each aligned block of 64 positions of a row, no expert is named by more than 36 routes.
All inputs are finite; a program needn't handle non-finite values.
Results may differ from the reference program's by a relative error of at most 0.028.
Values may be sent and summed in bfloat16 or wider, within the bound.
No kernel may reach another device: no remote copies, remote signals or barrier semaphores. Data moves between devices by JAX's collectives and lax.ppermute only.
A program may use at most 512 MiB of HBM per device.

```python
import math
import jax
import jax.numpy as jnp
import numpy as np
from jax import lax

D = 2048
H = 16
DN = 128
DR = 64
DV = 128
R = 512
FE = 1408
TOP = 6
SHARED = 2
MICRO = 2
SEQ = 1024
TOK_MB = 64
EXPERTS = 16
CAP = 36
ROWS = 4
N_FSDP = 16


def draw_lengths(key, part):
    key = jax.random.fold_in(key, 11)
    first, second = jax.random.split(key)
    drawn = jax.random.randint(first, (ROWS,), SEQ // 4, SEQ + 1, dtype=jnp.int32)
    chosen = jax.random.randint(second, (ROWS // MICRO,), 0, MICRO, dtype=jnp.int32)
    rows = jnp.arange(ROWS, dtype=jnp.int32)
    full = rows % MICRO == jnp.repeat(chosen, MICRO)
    return jnp.where(full, SEQ, drawn).astype(jnp.int32)


def levels(own_key, shape, pieces, smallest, high):
    def one(dim, blocks):
        heights = jax.random.uniform(jax.random.fold_in(jax.random.fold_in(own_key, 6), dim), (blocks,), jnp.float32, smallest / len(pieces), high / len(pieces))
        return jnp.repeat(jnp.exp(heights), shape[dim] // blocks).reshape((-1,) + (1,) * (len(shape) - dim - 1))

    level = one(*pieces[0])
    for cut in pieces[1:]:
        level = level * one(*cut)
    return level


def deal_out(rng, own, number, rows, number_of, top, bound, lean):
    sequence = jax.random.permutation(rng, number_of)
    packed, usual = portions_of(number_of, rows * top, bound, lean, True), portions_of(number_of, rows * top, bound, lean, False)
    places = jnp.arange(number_of)

    def named(sizes, offset_by):
        used = int((sizes > 0).sum())
        fixed = max(1, used // 4)
        shifted = fixed + (places - fixed + offset_by * (used - fixed)) % max(1, number_of - fixed)
        return jnp.zeros((number_of,), jnp.int32).at[sequence[jnp.where(places < fixed, places, shifted)]].set(jnp.asarray(sizes, jnp.int32))

    sizes = jnp.where(number % 4 == 0, named(packed, number // 4), named(usual, number - number // 4 - 1))
    mixed = jax.random.permutation(jax.random.fold_in(own, 3), number_of)
    source_of, sink = mixed[0:number_of // 2 * 2:2], mixed[1:number_of // 2 * 2:2]
    margin = jnp.minimum(sizes[source_of] - 1, bound - sizes[sink]) // 2
    margin = jnp.where((source_of == sequence[0]) | (sink == sequence[0]) | (sizes[sink] == 0), 0, jnp.maximum(margin, 0))
    shifted = jax.random.randint(jax.random.fold_in(own, 4), (number_of // 2,), 0, 1 << 20) % (margin + 1)
    sizes = sizes.at[source_of].add(-shifted).at[sink].add(shifted)
    items = jnp.searchsorted(jnp.cumsum(sizes), jnp.arange(rows * top), side="right").astype(jnp.int32)
    listing = items.reshape(top, rows).T
    listing = listing[jax.random.permutation(jax.random.fold_in(own, 1), rows)]
    offset_by = jax.random.randint(jax.random.fold_in(own, 2), (rows, 1), 0, top)
    return jnp.take_along_axis(listing, (jnp.arange(top)[None, :] + offset_by) % top, axis=1)


def portions_of(amount, total, limit, lean, full):
    loads = [(1 << 20) // math.isqrt(rank ** lean) + 1 for rank in range(1, amount + 1)]
    largest = limit if full else min(limit, max(-(-total // amount), total * loads[0] // sum(loads)))
    least = 1 if total - largest >= amount - 1 else 0
    counts, spare = [largest] + [least] * (amount - 1), total - largest - least * (amount - 1)
    while spare > 0:
        free = [i for i in range(1, amount) if counts[i] < largest] or [i for i in range(1, amount) if counts[i] < limit]
        whole, budget = sum([loads[i] for i in free]), spare
        for i in free:
            more = min(limit - counts[i], max(1, budget * loads[i] // whole), spare)
            counts[i] = counts[i] + more
            spare = spare - more
    return np.array(counts)


def normal_values(stream_key, dims, scale, reach, shards=(), kind=jnp.bfloat16):
    values = scale * jax.random.normal(stream_key, dims, jnp.float32)
    if shards:
        values = values * levels(stream_key, dims, shards, -0.22, 0.18)
    return jnp.clip(values, -reach, reach).astype(kind)


def setup_inputs(seed: int = 0) -> dict:
    seeds = jax.random.split(jax.random.key(seed), 19)
    hidden_in = normal_values(seeds[0], (ROWS, SEQ, D), 1.0, 6.0, ((0, 2), (1, 16)))
    cotangent = normal_values(seeds[1], (ROWS, SEQ, D), 1.0, 6.0, ((0, 2), (1, 16)))
    lengths = draw_lengths(jax.random.fold_in(seeds[18], 71), 0)
    routes_keys = jax.random.split(jax.random.fold_in(seeds[3], 1), ROWS * SEQ // TOK_MB)
    routes_turns = jax.random.permutation(jax.random.fold_in(seeds[3], 3), ROWS * SEQ // TOK_MB)
    routes = jax.vmap(lambda own, number: deal_out(jax.random.fold_in(seeds[3], 2), own, number, TOK_MB, EXPERTS, TOP, CAP, 2))(routes_keys, routes_turns).reshape((ROWS, SEQ, TOP))
    gate_values = jnp.clip(jnp.exp(math.log(1.0) - 1.3862944 * jax.random.uniform(seeds[4], (ROWS, SEQ, TOP), jnp.float32) ** levels(seeds[4], (ROWS, SEQ, TOP), ((0, 2), (1, 16)), -0.2, 0.2)), 0.25, 1.0)
    attn_gain = jnp.clip(1.0 + 0.1 * jax.random.normal(seeds[5], (D,), jnp.float32), 0.5, 1.5).astype(jnp.bfloat16)
    query_proj = normal_values(seeds[6], (D, H * (DN + DR)), D ** -0.5, 0.125, ((0, 16),))
    latent_proj = normal_values(seeds[7], (D, R + DR), D ** -0.5, 0.125, ((0, 16),))
    latent_gain = jnp.clip(1.0 + 0.1 * jax.random.normal(seeds[8], (R,), jnp.float32), 0.5, 1.5).astype(jnp.bfloat16)
    expand_proj = normal_values(seeds[9], (R, H * (DN + DV)), R ** -0.5, 0.25, ((0, 16),))
    output_proj = normal_values(seeds[10], (H * DV, D), (max(1, H * DV // 128)) ** -0.5, 1.5, ((0, 16),))
    ffn_gain = jnp.clip(1.0 + 0.1 * jax.random.normal(seeds[11], (D,), jnp.float32), 0.5, 1.5).astype(jnp.bfloat16)
    shared_gate = normal_values(seeds[12], (D, SHARED * FE), D ** -0.5, 0.125, ((0, 16),))
    shared_lift = normal_values(seeds[13], (D, SHARED * FE), D ** -0.5, 0.125, ((0, 16),))
    shared_down = normal_values(seeds[14], (SHARED * FE, D), (SHARED * FE) ** -0.5, 0.109375, ((0, 16),))
    expert_gate = normal_values(seeds[15], (EXPERTS, D, FE), D ** -0.5, 0.125, ((0, 16), (2, 2)))
    expert_lift = normal_values(seeds[16], (EXPERTS, D, FE), D ** -0.5, 0.125, ((0, 16), (2, 2)))
    expert_down = normal_values(seeds[17], (EXPERTS, FE, D), FE ** -0.5, 0.15625, ((0, 16), (1, 2)))
    return {"hidden_in": hidden_in, "cotangent": cotangent, "lengths": lengths, "routes": routes, "gate_values": gate_values, "attn_gain": attn_gain, "query_proj": query_proj, "latent_proj": latent_proj, "latent_gain": latent_gain, "expand_proj": expand_proj, "output_proj": output_proj, "ffn_gain": ffn_gain, "shared_gate": shared_gate, "shared_lift": shared_lift, "shared_down": shared_down, "expert_gate": expert_gate, "expert_lift": expert_lift, "expert_down": expert_down}


EPS = 1e-06
THETA = 10000.0
NEG = -1e+30

@jax.custom_vjp
def low(v):
    return lax.optimization_barrier(v.astype(jnp.bfloat16)).astype(jnp.float32)

@jax.custom_vjp
def low_back(v):
    return v

def low_keep(v):
    return (low(v), None)

def low_pass(kept, grad):
    return (grad,)

def back_keep(v):
    return (v, None)

def back_low(kept, grad):
    return (low(grad),)
low.defvjp(low_keep, low_pass)
low_back.defvjp(back_keep, back_low)

def product(left, right):
    return jnp.dot(left, right, precision=lax.Precision.HIGHEST)

def contract(form, left, right):
    return jnp.einsum(form, left, right, precision=lax.Precision.HIGHEST)

def rms_norm(value, gain):
    return value * lax.rsqrt(lax.optimization_barrier(jnp.mean(value * value, axis=-1, keepdims=True)) + EPS) * gain

def rope_tables(positions, width):
    half = width // 2
    freqs = THETA ** (-(2.0 * jnp.arange(half, dtype=jnp.float32)) / width)
    angles = positions.astype(jnp.float32)[:, None] * freqs[None, :]
    return (jnp.cos(angles), jnp.sin(angles))

def rotate(value, cosine, sine):
    half = value.shape[-1] // 2
    first = value[..., :half]
    second = value[..., half:]
    return jnp.concatenate([first * cosine - second * sine, second * cosine + first * sine], axis=-1)

def attend_block(block, latents, rotated, length, key_positions):
    query_lat, query_rot, query_pos = block
    scale = (DN + DR) ** (-0.5)
    scores = scale * (contract('qhr,kr->qhk', query_lat, latents) + contract('qhd,kd->qhk', query_rot, rotated))
    scores = low_back(scores)
    visible = (key_positions[None, None, :] <= query_pos[:, None, None]) & (key_positions[None, None, :] < length)
    scores = jnp.where(visible, scores, NEG)
    probs = low(jax.nn.softmax(scores, axis=-1))
    return contract('qhk,kr->qhr', probs, latents)

def expert_apply(item):
    rows, gate_w, lift_w, down_w = item
    gate_v = low_back(product(rows, gate_w))
    lift_v = low_back(product(rows, lift_w))
    hidden = low(jax.nn.silu(gate_v) * lift_v)
    return low(low_back(product(hidden, down_w)))

def route_slots(route_row):
    blocks = route_row.reshape(N_FSDP, TOK_MB * TOP)
    hits = (blocks[:, :, None] == jnp.arange(EXPERTS, dtype=jnp.int32)[None, None, :]).astype(jnp.int32)
    slot = lax.optimization_barrier(jnp.sum(hits * (jnp.cumsum(hits, axis=1) - 1), axis=2))
    source = jnp.arange(N_FSDP, dtype=jnp.int32)[:, None]
    return (blocks * (N_FSDP * CAP) + source * CAP + slot).reshape(SEQ * TOP).astype(jnp.int32)

def layer_row(inputs, params, length, route_row, gate_row):
    attn_gain, query_proj, latent_proj, latent_gain, expand_proj, output_proj, ffn_gain, shared_gate, shared_lift, shared_down, expert_gate, expert_lift, expert_down = params
    positions = jnp.arange(SEQ, dtype=jnp.int32)
    cosine, sine = rope_tables(positions, DR)
    normed = low(rms_norm(inputs, attn_gain))
    query = low_back(product(normed, query_proj)).reshape(SEQ, H, DN + DR)
    query_nope = low(query[:, :, :DN])
    query_rot = low(rotate(query[:, :, DN:], cosine[:, None, :], sine[:, None, :]))
    latent_all = low_back(product(normed, latent_proj))
    latents = low(rms_norm(latent_all[:, :R], latent_gain))
    rotated = low(rotate(latent_all[:, R:], cosine, sine))
    expand = expand_proj.reshape(R, H, DN + DV)
    query_lat = low(low_back(contract('shd,rhd->shr', query_nope, expand[:, :, :DN])))
    qblock = min(512, SEQ)
    count = SEQ // qblock

    def one_block(block):
        return attend_block(block, latents, rotated, length, positions)
    out_lat = lax.map(jax.checkpoint(one_block), (query_lat.reshape(count, qblock, H, R), query_rot.reshape(count, qblock, H, DR), positions.reshape(count, qblock)))
    out_lat = low(low_back(out_lat.reshape(SEQ, H, R)))
    heads_out = low(low_back(contract('shr,rhd->shd', out_lat, expand[:, :, DN:]))).reshape(SEQ, H * DV)
    residual = inputs + low_back(product(heads_out, output_proj))
    mixed = low(rms_norm(residual, ffn_gain))
    share_gate_v = low_back(product(mixed, shared_gate))
    share_lift_v = low_back(product(mixed, shared_lift))
    shared_out = product(low(jax.nn.silu(share_gate_v) * share_lift_v), shared_down)
    target = route_slots(route_row)
    copies = low_back(jnp.repeat(mixed, TOP, axis=0))
    buffer = jnp.zeros((EXPERTS * N_FSDP * CAP, D), jnp.float32).at[target].set(copies)
    results = lax.map(jax.checkpoint(expert_apply), (buffer.reshape(EXPERTS, N_FSDP * CAP, D), expert_gate, expert_lift, expert_down))
    picked = results.reshape(EXPERTS * N_FSDP * CAP, D)[target].reshape(SEQ, TOP, D)
    routed = lax.optimization_barrier(jnp.sum(gate_row[:, :, None] * picked, axis=1))
    return residual + shared_out + routed

def reference(hidden_in, cotangent, lengths, routes, gate_values, attn_gain, query_proj, latent_proj, latent_gain, expand_proj, output_proj, ffn_gain, shared_gate, shared_lift, shared_down, expert_gate, expert_lift, expert_down):
    params = tuple((item.astype(jnp.float32) for item in (attn_gain, query_proj, latent_proj, latent_gain, expand_proj, output_proj, ffn_gain, shared_gate, shared_lift, shared_down, expert_gate, expert_lift, expert_down)))
    start = tuple((jnp.zeros_like(item) for item in params))

    def one_row(totals, item):
        inputs, grad_row, length, route_row, gate_row = item

        def forward(values, weights):
            return layer_row(values, weights, length, route_row, gate_row.astype(jnp.float32))
        result, pullback = jax.vjp(forward, inputs.astype(jnp.float32), params)
        keep = (jnp.arange(SEQ, dtype=jnp.int32) < length)[:, None]
        grad_in, grad_params = pullback(jnp.where(keep, grad_row.astype(jnp.float32), 0.0))
        totals = tuple((left + right for left, right in zip(totals, grad_params)))
        return (totals, (result.astype(jnp.bfloat16), grad_in.astype(jnp.bfloat16)))
    totals, outs = lax.scan(one_row, start, (hidden_in, cotangent, lengths, routes, gate_values))
    return (outs[0], outs[1], totals[0], totals[1], totals[2], totals[3], totals[4], totals[5], totals[6], totals[7], totals[8], totals[9], totals[10], totals[11], totals[12])
```

```python
import jax
import jax.numpy as jnp
from jax import lax
from jax.sharding import PartitionSpec as P

H = 16
DN = 128
DR = 64
DV = 128
R = 512
TOP = 6
MICRO = 2

EPS = 1e-06
THETA = 10000.0
NEG = -1e30
F32 = jnp.float32
BF16 = jnp.bfloat16


def contract(form, left, right):
    return jnp.einsum(form, left, right, preferred_element_type=F32)


def rms_forward(value, gain):
    factor = lax.rsqrt(jnp.mean(value * value, axis=-1, keepdims=True) + EPS)
    return (value * factor * gain, factor)


def rms_backward(value, factor, gain, grad):
    scaled = grad * gain
    inner = jnp.mean(value * scaled, axis=-1, keepdims=True)
    return (
        factor * scaled - value * factor * factor * factor * inner,
        jnp.sum(grad * value * factor, axis=0),
    )


def rope_tables(positions, width):
    half = width // 2
    freqs = THETA ** (-(2.0 * jnp.arange(half, dtype=F32)) / width)
    angles = positions.astype(F32)[:, None] * freqs[None, :]
    return (jnp.cos(angles), jnp.sin(angles))


def rotate(value, cosine, sine):
    half = value.shape[-1] // 2
    first = value[..., :half]
    second = value[..., half:]
    return jnp.concatenate(
        [first * cosine - second * sine, second * cosine + first * sine], axis=-1
    )


def rotate_back(grad, cosine, sine):
    half = grad.shape[-1] // 2
    first = grad[..., :half]
    second = grad[..., half:]
    return jnp.concatenate(
        [first * cosine + second * sine, second * cosine - first * sine], axis=-1
    )


def silu_slope(value):
    sigma = jax.nn.sigmoid(value)
    return sigma * (1.0 + value * (1.0 - sigma))


def partners(devices, k, i, j):
    outer = devices // 4
    return [
        (d, ((d // 4 + k) % outer) * 4 + ((d % 4) ^ (2 * i + j))) for d in range(devices)
    ]


def pull(value, devices, k, i, j):
    perm = [(there, here) for here, there in partners(devices, k, i, j)]
    return lax.ppermute(value, "fsdp", perm)


def push(value, devices, k, i, j):
    return lax.ppermute(value, "fsdp", partners(devices, k, i, j))


def outer_order(outer):
    near = []
    for k in range(1, outer):
        near.append((min(k, outer - k), k))
    return [k for _, k in sorted(near)]


def gather_blocks(block, devices):
    outer = devices // 4
    order = [0] + outer_order(outer)
    base = {0: block}
    for k in order[1:]:
        base[k] = pull(block, devices, k, 0, 0)
    held = {}
    for k in order:
        held[k, 0, 0] = base[k]
        held[k, 0, 1] = pull(base[k], devices, 0, 0, 1)
        held[k, 1, 0] = pull(base[k], devices, 0, 1, 0)
    for place, k in enumerate(order):
        if place % 2 == 0:
            held[k, 1, 1] = pull(held[k, 0, 1], devices, 0, 1, 0)
        else:
            held[k, 1, 1] = pull(held[k, 1, 0], devices, 0, 0, 1)
    return [held[k, i, j] for k in range(outer) for i in (0, 1) for j in (0, 1)]


def total(first, *others):
    value = first.astype(F32)
    for item in others:
        value = value + item.astype(F32)
    return value


def scatter_blocks(blocks, devices):
    outer = devices // 4
    order = outer_order(outer)[::-1] + [0]
    held = {}
    for k in range(outer):
        for i in (0, 1):
            for j in (0, 1):
                held[k, i, j] = blocks[4 * k + 2 * i + j]
    for place, k in enumerate(order):
        if place % 2 == 0:
            held[k, 0, 1] = total(held[k, 0, 1], push(held[k, 1, 1], devices, 0, 1, 0)).astype(BF16)
        else:
            held[k, 1, 0] = total(held[k, 1, 0], push(held[k, 1, 1], devices, 0, 0, 1)).astype(BF16)
    sums = {}
    for k in order:
        sums[k] = total(
            held[k, 0, 0],
            push(held[k, 0, 1], devices, 0, 0, 1),
            push(held[k, 1, 0], devices, 0, 1, 0),
        )
    return total(sums[0], *[push(sums[k].astype(BF16), devices, k, 0, 0) for k in order[:-1]])


def rep_pull(value, count, step):
    return lax.ppermute(value, "rep", [((d + step) % count, d) for d in range(count)])


def rep_parts(value, count):
    return [value] + [rep_pull(value, count, step) for step in range(1, count)]


def rep_total(parts, count):
    value = parts[0].astype(F32)
    for step in range(1, count):
        perm = [(d, (d + step) % count) for d in range(count)]
        value = value + lax.ppermute(parts[step], "rep", perm).astype(F32)
    return value


def body(
    hidden_in,
    cotangent,
    lengths,
    routes,
    gate_values,
    attn_gain,
    query_proj,
    latent_proj,
    latent_gain,
    expand_proj,
    output_proj,
    ffn_gain,
    shared_gate,
    shared_lift,
    shared_down,
    expert_gate,
    expert_lift,
    expert_down,
):
    tok = hidden_in.shape[1]
    width = hidden_in.shape[2]
    n = lax.axis_size("fsdp")
    reps = lax.axis_size("rep")
    me = lax.axis_index("fsdp")
    rep = lax.axis_index("rep")
    outer = n // 4
    seq = tok * n
    capacity = min(tok, 3 * tok * TOP // (2 * n))
    split = max(1, n // H)
    scale = (DN + DR) ** (-0.5)
    rows = width // n

    slots = jnp.arange(n, dtype=jnp.int32)
    abs_of_rel = ((me // 4 + slots // 4) % outer) * 4 + ((me % 4) ^ (slots % 4))
    rel_of_abs = ((slots // 4 - me // 4) % outer) * 4 + ((slots % 4) ^ (me % 4))
    rep_order = (jnp.arange(reps, dtype=jnp.int32) - rep) % reps
    own_pos = me * tok + jnp.arange(tok, dtype=jnp.int32)
    pos = (abs_of_rel[:, None] * tok + jnp.arange(tok, dtype=jnp.int32)[None, :]).reshape(seq)
    cosine, sine = rope_tables(pos, DR)

    def all_to_all(value):
        return lax.all_to_all(value, "fsdp", split_axis=0, concat_axis=0, tiled=True)

    def rep_slice(value, axis):
        size = value.shape[axis] // reps
        return lax.dynamic_slice_in_dim(value, rep * size, size, axis)

    def rep_join(value, axis):
        parts = jnp.take(jnp.stack(rep_parts(value, reps)), rep_order, axis=0)
        return jnp.concatenate([parts[i] for i in range(reps)], axis=axis)

    def reshard(value):
        return rep_join(all_to_all(rep_slice(value, 1)), 1)

    def unreshard(value):
        size = value.shape[1] // reps
        parts = [
            lax.dynamic_slice_in_dim(value, ((rep + step) % reps) * size, size, 1).astype(BF16)
            for step in range(reps)
        ]
        parts[0] = lax.dynamic_slice_in_dim(value, rep * size, size, 1)
        return rep_join(all_to_all(rep_total(parts, reps).astype(BF16)), 1).astype(F32)

    def by_head(value):
        return jnp.repeat(value, split, axis=0) if split > 1 else value

    hidden_all = [
        jnp.concatenate(gather_blocks(hidden_in[m], n), axis=0) for m in range(MICRO)
    ]

    gains = jnp.stack(
        [attn_gain, ffn_gain, jnp.pad(latent_gain, (0, rows - latent_gain.shape[0]))]
    )
    small = jnp.concatenate(
        [rep_slice(latent_proj.T, 0), jnp.pad(gains, ((0, 13), (0, 0)))], axis=0
    )
    small_all = jnp.take(jnp.stack(gather_blocks(small, n)), rel_of_abs, axis=0)
    part = small.shape[0] - 16
    latent_t = rep_join(
        jnp.transpose(small_all[:, :part], (1, 0, 2)).reshape(part, width), 0
    )
    attn_gain_f = small_all[:, part].reshape(width).astype(F32)
    ffn_gain_f = small_all[:, part + 1].reshape(width).astype(F32)
    latent_gain_f = small_all[:, part + 2, : latent_gain.shape[0]].reshape(R).astype(F32)

    query_w = reshard(
        by_head(jnp.transpose(query_proj.reshape(rows, H, DN + DR), (1, 0, 2)))
    ).reshape(width, DN + DR)
    expand_w = reshard(
        by_head(jnp.transpose(expand_proj.reshape(R // n, H, DN + DV), (1, 0, 2)))
    ).reshape(R, DN + DV)
    in_w = jnp.concatenate(
        [query_w[:, :DN], latent_t[:R].T, query_w[:, DN:], latent_t[R:].T], axis=1
    )

    att = []
    heads_local = []
    for m in range(MICRO):
        length = lengths[m]
        value = hidden_all[m].astype(F32)
        normed, factor = rms_forward(value, attn_gain_f)
        normed = normed.astype(BF16)
        mixed_in = contract("td,dj->tj", normed, in_w)
        latent = mixed_in[:, DN : DN + R]
        latent_norm, latent_factor = rms_forward(latent, latent_gain_f)
        latent_low = latent_norm.astype(BF16)
        q_rot = rotate(mixed_in[:, DN + R : DN + R + DR], cosine, sine)
        k_rot = rotate(mixed_in[:, DN + R + DR :], cosine, sine)
        kv = contract("tr,rj->tj", latent_low, expand_w)
        query = jnp.concatenate([mixed_in[:, :DN], q_rot], axis=1).astype(BF16)
        key = jnp.concatenate([kv[:, :DN], k_rot], axis=1).astype(BF16)
        val = kv[:, DN:].astype(BF16)
        visible = (pos[None, :] <= pos[:, None]) & (pos[None, :] < length)
        scores = jnp.where(visible, scale * contract("td,sd->ts", query, key), NEG)
        peak = jnp.max(scores, axis=-1, keepdims=True)
        raised = jnp.exp(scores - peak)
        probs = raised / jnp.sum(raised, axis=-1, keepdims=True)
        probs_low = probs.astype(BF16)
        out = contract("ts,sd->td", probs_low, val).astype(BF16)
        out = jnp.take(out.reshape(n, tok, DV), rel_of_abs, axis=0)
        out = all_to_all(out)[::split]
        heads_out = jnp.transpose(out, (1, 0, 2)).reshape(tok, n, H * DV // n)
        heads_local.append(jnp.take(heads_out, abs_of_rel, axis=1).reshape(tok, H * DV))
        att.append((value, factor, normed, latent[:tok], latent_factor[:tok], latent_low,
                    query, key, val, probs, probs_low))

    cols = width // reps
    out_blocks = gather_blocks(rep_slice(output_proj, 1), n)
    out_parts = rep_parts(jnp.concatenate(out_blocks, axis=0), reps)

    def columns(step):
        return ((rep + step) % reps) * cols

    grad_rows = []
    grad_all = []
    for m in range(MICRO):
        grad_rows.append(
            jnp.where((own_pos < lengths[m])[:, None], cotangent[m], jnp.zeros_like(cotangent[m]))
        )
        grad_all.append(jnp.concatenate(gather_blocks(grad_rows[m], n), axis=0))

    shared_in = jnp.concatenate(
        [
            jnp.transpose(shared_gate.reshape(rows, n, -1), (1, 0, 2)),
            jnp.transpose(shared_lift.reshape(rows, n, -1), (1, 0, 2)),
        ],
        axis=2,
    )
    units = shared_in.shape[2] // 2
    shared_in = reshard(shared_in).reshape(width, 2 * units)
    gate_parts = rep_parts(jnp.swapaxes(expert_gate[0], 0, 1), reps)
    lift_parts = rep_parts(jnp.swapaxes(expert_lift[0], 0, 1), reps)
    down_parts = rep_parts(expert_down[0], reps)

    dense_gate = jnp.sum(
        jnp.where(routes[..., None] == slots, gate_values[..., None], 0.0), axis=2
    )
    arrived_gate = all_to_all(jnp.transpose(dense_gate, (2, 0, 1)))
    arrived_gate = jnp.take(arrived_gate, abs_of_rel, axis=0)

    merge = 1
    while (merge * capacity) % 16:
        merge *= 2
    groups = n // merge
    span = merge * tok
    room = merge * capacity
    upper = (jnp.arange(span)[:, None] <= jnp.arange(span)[None, :]).astype(BF16)

    outputs = []
    input_grads = []
    part_ffn = 0.0
    keep = []
    for m in range(MICRO):
        hidden = hidden_in[m].astype(F32)
        residual = jnp.zeros((tok, width), F32)
        for step in range(reps):
            share = contract("tj,jd->td", heads_local[m], out_parts[step])
            residual = lax.dynamic_update_slice(residual, share, (0, columns(step)))
        residual = hidden + residual
        mixed, inv_second = rms_forward(residual, ffn_gain_f)
        mixed_all = jnp.concatenate(gather_blocks(mixed.astype(BF16), n), axis=0)

        gate_here = arrived_gate[:, m].reshape(groups, span)
        hit = gate_here > 0.0
        place = contract("gt,ts->gs", hit.astype(BF16), upper).astype(jnp.int32) - 1
        chosen = hit[:, None, :] & (
            place[:, None, :] == jnp.arange(room, dtype=jnp.int32)[None, :, None]
        )
        pick = chosen.astype(BF16)
        row_gate = jnp.sum(jnp.where(chosen, gate_here[:, None, :], 0.0), axis=2).reshape(-1, 1)

        def select(value):
            return contract("gct,gtd->gcd", pick, value.reshape(groups, span, width)).reshape(
                groups * room, width
            )

        def spread(value):
            return contract("gct,gcd->gtd", pick, value.reshape(groups, room, width)).reshape(
                seq, width
            )

        arrived = select(mixed_all).astype(BF16)
        back = (row_gate * select(grad_all[m])).astype(BF16)

        share_v = contract("td,df->tf", mixed_all, shared_in)
        share_g, share_u = share_v[:, :units], share_v[:, units:]
        shared_hidden = (jax.nn.silu(share_g) * share_u).astype(BF16)
        grad_shared = contract("td,fd->tf", grad_all[m], shared_down)
        grad_sgu = jnp.concatenate(
            [
                (grad_shared * share_u * silu_slope(share_g)).astype(BF16),
                (grad_shared * jax.nn.silu(share_g)).astype(BF16),
            ],
            axis=1,
        )

        expert_out = 0.0
        grad_arrived = 0.0
        eh, eg, eu = [], [], []
        for step in range(reps):
            gate_v = contract("cd,fd->cf", arrived, gate_parts[step])
            lift_v = contract("cd,fd->cf", arrived, lift_parts[step])
            grad_eh = contract("cd,fd->cf", back, down_parts[step])
            eh.append((jax.nn.silu(gate_v) * lift_v).astype(BF16))
            eg.append((grad_eh * lift_v * silu_slope(gate_v)).astype(BF16))
            eu.append((grad_eh * jax.nn.silu(gate_v)).astype(BF16))
            grad_arrived = grad_arrived + (
                contract("cf,fd->cd", eg[step], gate_parts[step])
                + contract("cf,fd->cd", eu[step], lift_parts[step])
            )
        grad_mixed_part = (
            spread(grad_arrived.astype(BF16)) + contract("tf,df->td", grad_sgu, shared_in)
        ).astype(BF16)
        grad_mixed = scatter_blocks(
            [grad_mixed_part[s * tok : (s + 1) * tok] for s in range(n)], n
        )
        for step in range(reps):
            expert_out = expert_out + contract("cf,fd->cd", eh[step], down_parts[step])
        out_part = (
            spread((row_gate * expert_out.astype(BF16).astype(F32)).astype(BF16))
            + contract("tf,fd->td", shared_hidden, shared_down)
        ).astype(BF16)
        routed = scatter_blocks([out_part[s * tok : (s + 1) * tok] for s in range(n)], n)
        outputs.append((residual + routed).astype(BF16))

        grad_res, ffn = rms_backward(residual, inv_second, ffn_gain_f, grad_mixed)
        part_ffn = part_ffn + ffn
        grad_res = grad_res + grad_rows[m].astype(F32)
        grad_res_low = grad_res.astype(BF16)
        grad_heads = 0.0
        for step in range(reps):
            piece = lax.dynamic_slice_in_dim(grad_res_low, columns(step), cols, 1)
            grad_heads = grad_heads + contract("td,jd->tj", piece, out_parts[step])
        keep.append((arrived, back, eh, eg, eu, mixed_all, shared_hidden, grad_sgu,
                     grad_res, grad_res_low, grad_heads.astype(BF16)))

    def joined(index):
        return jnp.concatenate([item[index] for item in keep], axis=0)

    def joined_step(index, step):
        return jnp.concatenate([item[index][step] for item in keep], axis=0)

    all_ar, all_ba = joined(0), joined(1)

    def expert_total(form, index, other):
        parts = [contract(form, joined_step(index, step), other) for step in range(reps)]
        return rep_total([parts[0]] + [item.astype(BF16) for item in parts[1:]], reps)

    grad_expert_gate = jnp.swapaxes(expert_total("cf,cd->fd", 3, all_ar), 0, 1)[None]
    grad_expert_lift = jnp.swapaxes(expert_total("cf,cd->fd", 4, all_ar), 0, 1)[None]
    grad_expert_down = expert_total("cf,cd->fd", 2, all_ba)[None]

    all_mx = joined(5)
    grad_shared_in = unreshard(
        contract("td,tf->df", all_mx, joined(7)).reshape(n, rows, 2 * units)
    )
    grad_shared_gate = jnp.transpose(grad_shared_in[:, :, :units], (1, 0, 2)).reshape(rows, -1)
    grad_shared_lift = jnp.transpose(grad_shared_in[:, :, units:], (1, 0, 2)).reshape(rows, -1)
    down_sum = contract("tf,td->fd", joined(6), jnp.concatenate(grad_all, axis=0))
    grad_shared_down = down_sum + sum(
        rep_pull(down_sum.astype(BF16), reps, step).astype(F32) for step in range(1, reps)
    )

    grad_in_w = 0.0
    grad_expand_w = 0.0
    part_attn = 0.0
    part_latent = 0.0
    grad_kvs = []
    normed_first = []
    for m in range(MICRO):
        (value, factor, normed, latent, latent_factor, latent_low,
         query, key, val, probs, probs_low) = att[m]
        grad_heads = jnp.take(keep[m][10].reshape(tok, n, H * DV // n), rel_of_abs, axis=1)
        grad_heads = by_head(jnp.transpose(grad_heads.reshape(tok, H, DV), (1, 0, 2)))
        grad_heads = jnp.take(all_to_all(grad_heads), abs_of_rel, axis=0).reshape(seq, DV)
        if split > 1:
            grad_heads = jnp.where(me % split == 0, grad_heads, jnp.zeros_like(grad_heads))
        grad_probs = contract("td,sd->ts", grad_heads, val)
        grad_scores = (
            probs * (grad_probs - jnp.sum(probs * grad_probs, axis=-1, keepdims=True))
        ).astype(BF16)
        grad_query = scale * contract("ts,sd->td", grad_scores, key)
        grad_key = scale * contract("ts,td->sd", grad_scores, query)
        grad_val = contract("ts,td->sd", probs_low, grad_heads)
        grad_query = jnp.concatenate(
            [grad_query[:, :DN], rotate_back(grad_query[:, DN:], cosine, sine)], axis=1
        ).astype(BF16)
        grad_kv = jnp.concatenate([grad_key[:, :DN], grad_val], axis=1).astype(BF16)
        grad_latent_part = jnp.concatenate(
            [contract("tj,rj->tr", grad_kv, expand_w), grad_key[:, DN:]], axis=1
        ).astype(BF16)
        grad_latent = scatter_blocks(
            [grad_latent_part[s * tok : (s + 1) * tok] for s in range(n)], n
        )
        grad_normed_part = contract("tj,dj->td", grad_query, query_w)
        part_attn = part_attn + jnp.sum(grad_normed_part * value * factor, axis=0)
        grad_normed_part = grad_normed_part.astype(BF16)
        grad_normed = scatter_blocks(
            [grad_normed_part[s * tok : (s + 1) * tok] for s in range(n)], n
        )
        grad_in_w = grad_in_w + contract("td,tj->dj", normed, grad_query)
        grad_expand_w = grad_expand_w + contract("tr,tj->rj", latent_low, grad_kv)

        grad_c, latent_sum = rms_backward(
            latent, latent_factor, latent_gain_f, grad_latent[:, :R]
        )
        part_latent = part_latent + latent_sum
        grad_krope = rotate_back(grad_latent[:, R:], cosine[:tok], sine[:tok])
        grad_kva = jnp.concatenate([grad_c, grad_krope], axis=1).astype(BF16)
        grad_kvs.append(grad_kva)
        grad_local = contract("tj,jd->td", grad_kva, latent_t)
        part_attn = part_attn + jnp.sum(grad_local * value[:tok] * factor[:tok], axis=0)
        grad_first, _ = rms_backward(
            value[:tok], factor[:tok], attn_gain_f, grad_normed + grad_local
        )
        input_grads.append((grad_first + keep[m][8]).astype(BF16))

    grad_query_proj = jnp.transpose(
        unreshard(grad_in_w.reshape(n, rows, DN + DR))[::split], (1, 0, 2)
    ).reshape(rows, H * (DN + DR))
    grad_expand_proj = jnp.transpose(
        unreshard(grad_expand_w.reshape(n, R // n, DN + DV))[::split], (1, 0, 2)
    ).reshape(R // n, H * (DN + DV))

    kv_blocks = gather_blocks(jnp.concatenate(grad_kvs, axis=0), n)
    latent_total = 0.0
    for m in range(MICRO):
        kv_all = jnp.concatenate([item[m * tok : (m + 1) * tok] for item in kv_blocks], axis=0)
        piece = lax.dynamic_slice_in_dim(att[m][2], me * rows, rows, 1)
        latent_total = latent_total + contract("tj,td->jd", kv_all, piece)
    latent_total = latent_total + sum(
        rep_pull(latent_total.astype(BF16), reps, step).astype(F32) for step in range(1, reps)
    )
    grad_latent_proj = latent_total.T

    all_ho = jnp.concatenate(heads_local, axis=0)
    all_gr = joined(9)
    shares = []
    for step in range(reps):
        piece = lax.dynamic_slice_in_dim(all_gr, columns(step), cols, 1)
        shares.append(contract("tj,td->jd", all_ho, piece))
    out_total = rep_total([shares[0]] + [item.astype(BF16) for item in shares[1:]], reps)
    out_total = out_total.astype(BF16).reshape(n, rows, cols)
    out_total = scatter_blocks([out_total[s] for s in range(n)], n).astype(BF16)
    grad_output_proj = rep_join(out_total, 1).astype(F32)

    gain_parts = jnp.stack(
        [
            part_attn.reshape(n, rows),
            part_ffn.reshape(n, rows),
            jnp.pad(part_latent.reshape(n, R // n), ((0, 0), (0, rows - R // n))),
        ],
        axis=1,
    )
    gain_sum = jnp.sum(all_to_all(gain_parts), axis=0)
    gain_sum = gain_sum + sum(rep_pull(gain_sum, reps, step) for step in range(1, reps))

    return (
        jnp.stack(outputs),
        jnp.stack(input_grads),
        gain_sum[0],
        grad_query_proj,
        grad_latent_proj,
        gain_sum[2, : R // n],
        grad_expand_proj,
        grad_output_proj,
        gain_sum[1],
        grad_shared_gate,
        grad_shared_lift,
        grad_shared_down,
        grad_expert_gate,
        grad_expert_lift,
        grad_expert_down,
    )


def solution(mesh):
    in_specs = (
        P("rep", "fsdp", None),
        P("rep", "fsdp", None),
        P("rep"),
        P("rep", "fsdp", None),
        P("rep", "fsdp", None),
        P("fsdp"),
        P("fsdp", None),
        P("fsdp", None),
        P("fsdp"),
        P("fsdp", None),
        P("fsdp", None),
        P("fsdp"),
        P("fsdp", None),
        P("fsdp", None),
        P("fsdp", None),
        P("fsdp", None, "rep"),
        P("fsdp", None, "rep"),
        P("fsdp", "rep", None),
    )
    out_specs = (
        P("rep", "fsdp", None),
        P("rep", "fsdp", None),
        P("fsdp"),
        P("fsdp", None),
        P("fsdp", None),
        P("fsdp"),
        P("fsdp", None),
        P("fsdp", None),
        P("fsdp"),
        P("fsdp", None),
        P("fsdp", None),
        P("fsdp", None),
        P("fsdp", None, "rep"),
        P("fsdp", None, "rep"),
        P("fsdp", "rep", None),
    )
    return jax.shard_map(body, mesh=mesh, in_specs=in_specs, out_specs=out_specs, check_vma=False)
```

```python
import functools

import jax
import jax.numpy as jnp
from jax import lax
from jax.experimental import pallas as pl
from jax.experimental.pallas import tpu as pltpu
from jax.sharding import PartitionSpec as P

H = 16
DN = 128
DR = 64
DV = 128
R = 512
TOP = 6
MICRO = 2

EPS = 1e-06
THETA = 10000.0
F32 = jnp.float32
BF16 = jnp.bfloat16


def contract(form, left, right):
    return jnp.einsum(form, left, right, preferred_element_type=F32)


def rms_forward(value, gain):
    factor = lax.rsqrt(jnp.mean(value * value, axis=-1, keepdims=True) + EPS)
    return (value * factor * gain, factor)


def rms_backward(value, factor, gain, grad):
    scaled = grad * gain
    inner = jnp.mean(value * scaled, axis=-1, keepdims=True)
    return (
        factor * scaled - value * factor * factor * factor * inner,
        jnp.sum(grad * value * factor, axis=0),
    )


def rotate_back(grad, cosine, sine):
    half = grad.shape[-1] // 2
    first = grad[..., :half]
    second = grad[..., half:]
    return jnp.concatenate(
        [first * cosine + second * sine, second * cosine - first * sine], axis=-1
    )


def swapped(weight):
    half = weight.shape[1] // 2
    return [-weight[:, half:], weight[:, :half]]


def named(function):
    def scoped(name, *args):
        with jax.named_scope(name):
            return function(*args)

    return scoped


def near_first(outer):
    return [0] + [k for _, k in sorted((min(k, outer - k), k) for k in range(1, outer))]


def partners(devices, q, k):
    outer = devices // 4
    return [(d, ((d // 4 + k) % outer) * 4 + ((d % 4) ^ q)) for d in range(devices)]


def pull(value, devices, q, k=0):
    perm = [(there, here) for here, there in partners(devices, q, k)]
    return lax.ppermute(value, "fsdp", perm)


def push(value, devices, q, k=0):
    return lax.ppermute(value, "fsdp", partners(devices, q, k))


def order_after(values, marks):
    values, marks = list(values), list(marks)
    if not marks:
        return values, marks
    both = lax.optimization_barrier(tuple(values + marks))
    return list(both[: len(values)]), list(both[len(values) :])


def total(first, *others):
    value = first.astype(F32)
    for item in others:
        value = value + item.astype(F32)
    return value


@named
def gather_small(block, devices, cross_marks=(), last_marks=()):
    outer = devices // 4
    half = outer // 2
    base = jnp.stack([block] + [pull(block, devices, 0, k) for k in near_first(outer)[1:]])
    (sent,), cross_marks = order_after([base], cross_marks)
    one = pull(sent, devices, 1)
    two = pull(sent, devices, 2)
    (low, high), last_marks = order_after([one[:half], two[half:]], last_marks)
    low, high = pull(low, devices, 2), pull(high, devices, 1)
    return [base, one, two, low, high], cross_marks, last_marks


@named
def scatter_small_last(pieces, devices):
    base, one, two, low, high = pieces
    half = devices // 8
    low = push(low, devices, 2)
    high = push(high, devices, 1)
    zero = (0,) * one.ndim
    one = lax.dynamic_update_slice(one, total(one[:half], low).astype(BF16), zero)
    two = lax.dynamic_update_slice(
        two, total(two[half:], high).astype(BF16), (half,) + zero[1:]
    )
    return base, one, two


@named
def scatter_small_rest(pieces, devices, marks=()):
    base, one, two = pieces
    outer = devices // 4
    base = total(base, push(one, devices, 1), push(two, devices, 2))
    (sent,), marks = order_after([base[1:].astype(BF16)], marks)
    order = near_first(outer)
    return total(
        base[0], *[push(sent[i - 1], devices, 0, order[i]) for i in range(1, outer)]
    ), marks


@named
def gather_tree(block, devices, marks):
    outer = devices // 4
    half, part = outer // 2, outer // 4
    marks = [list(items) for items in marks]
    held = [block]
    for k in near_first(outer)[1:]:
        held.append(pull(block, devices, 0, k))
    pieces = [[], [], [], []]
    before = []
    for place, base in enumerate((held[:half], held[half:])):
        base = jnp.stack(base)
        if place == 0:
            (base,), marks[0] = order_after([base], marks[0])
        else:
            (base,), given = order_after([base], before + marks[1])
            pieces[1], pieces[2], marks[1] = given[0:1], given[1:2], given[2:]
        one = pull(base, devices, 1)
        two = pull(base, devices, 2)
        before = [one, two]
        low, high = one[:part], two[part:]
        if place:
            (low, high), given = order_after([low, high], pieces[3] + marks[2])
            pieces[3], marks[2] = given[:2], given[2:]
        last = [pull(low, devices, 2), pull(high, devices, 1)]
        for q, items in enumerate(([base], [one], [two], last)):
            pieces[q] += items
    return sum(pieces, []), marks


@named
def scatter_tree_last(pieces, devices):
    part = devices // 16
    halves = []
    for here in (1, 0):
        base, one, two = pieces[here], pieces[2 + here], pieces[4 + here]
        low, high = pieces[6 + 2 * here : 8 + 2 * here]
        low = push(low, devices, 2)
        high = push(high, devices, 1)
        zero = (0,) * one.ndim
        one = lax.dynamic_update_slice(one, total(one[:part], low).astype(BF16), zero)
        two = lax.dynamic_update_slice(
            two, total(two[part:], high).astype(BF16), (part,) + zero[1:]
        )
        halves.append((base, one, two))
    return halves


@named
def scatter_tree_cross(halves, devices):
    bases = []
    for base, one, two in halves:
        one = push(one, devices, 1)
        two = push(two, devices, 2)
        bases.append([total(base[i], one[i], two[i]) for i in range(base.shape[0])])
    return bases


@named
def scatter_tree_rest(bases, devices, marks=()):
    outer = devices // 4
    order = near_first(outer)
    sent, marks = order_after(
        [item.astype(BF16) for item in bases[0] + bases[1][1:]], marks
    )
    steps = order[outer // 2 :] + order[1 : outer // 2]
    arrived = [push(item, devices, 0, k) for item, k in zip(sent, steps)]
    return total(bases[1][0], *arrived), marks


def order_bases(bases, marks):
    values, marks = order_after(bases[0] + bases[1], marks)
    half = len(bases[0])
    return [values[:half], values[half:]], marks


def tree_sizes(devices):
    outer = devices // 4
    return [outer // 2] * 6 + [outer // 4] * 4


def small_split(value):
    count = value.shape[0] // 4
    half = count // 2
    cuts = (0, count, 2 * count, 3 * count, 3 * count + half, 4 * count)
    return [value[a:b] for a, b in zip(cuts, cuts[1:])]


LIMIT = 58 * 1024 * 1024


def mm(left, right):
    return jnp.dot(left, right, preferred_element_type=F32)


def mm_t(left, right):
    return lax.dot_general(left, right, (((1,), (1,)), ((), ())), preferred_element_type=F32)


def t_mm(left, right):
    return lax.dot_general(left, right, (((0,), (0,)), ((), ())), preferred_element_type=F32)


TREE = 10


def call(kernel, out_shape, places, scratch, flops, moved, *args, outs=None, aliases=None, marks=()):
    count = len(args)

    def without_marks(*refs):
        kernel(*refs[:count], *refs[count + len(marks) :])

    outs = outs or [pltpu.VMEM] * len(out_shape)
    places = list(places) + [pl.ANY] * len(marks)
    return pl.pallas_call(
        without_marks,
        out_shape=out_shape,
        in_specs=[pl.BlockSpec(memory_space=place) for place in places],
        out_specs=tuple(pl.BlockSpec(memory_space=place) for place in outs),
        input_output_aliases=aliases or {},
        scratch_shapes=scratch,
        compiler_params=pltpu.CompilerParams(vmem_limit_bytes=LIMIT),
        cost_estimate=pl.CostEstimate(flops=flops, bytes_accessed=moved, transcendentals=0),
    )(*args, *marks)


def sds(shape, dtype=BF16):
    return jax.ShapeDtypeStruct(shape, dtype)


def tree_copies(pieces, whole, sems, m, out=False):
    tok = whole.shape[1]
    copies, at = [], 0
    for place, piece in enumerate(pieces):
        count = piece.shape[0]
        ends = piece.at[:, pl.ds(m * tok, tok)], whole.at[pl.ds(at, count)]
        if out:
            ends = ends[::-1]
        copies.append(pltpu.make_async_copy(*ends, sems.at[place]))
        at += count
    return copies


def run(copies):
    for copy in copies:
        copy.start()
    for copy in copies:
        copy.wait()


def rows_of(whole, start, count):
    value = whole[pl.ds(start, count)]
    return value.reshape(count * value.shape[1], value.shape[2])


def attend_kernel(
    order, length, *refs,
):
    pieces = refs[:TREE]
    (query_w, latent_w, expand_w, gain, latent_gain, turn, pos_q, pos_k,
     out, q_nope, q_rot, k_nope, k_rot, val, latent_n, probs, factor, latent_own,
     x, sems) = refs[TREE:]
    blocks, tok, width = x.shape
    quarter = blocks // 4
    span = quarter * tok
    scale = (DN + DR) ** (-0.5)
    lane = lax.broadcasted_iota(jnp.int32, (1, 128), 1)
    loads = [tree_copies(pieces, x, sems, m) for m in range(MICRO)]
    for copy in loads[0]:
        copy.start()
    for m in range(MICRO):
        for copy in loads[m]:
            copy.wait()

        @pl.loop(0, 4)
        def _(g):
            here = pl.ds(pl.multiple_of(g * span, span), span)
            value = rows_of(x, g * quarter, quarter).astype(F32)
            inv = lax.rsqrt(jnp.mean(value * value, axis=-1, keepdims=True) + EPS)
            factor[m, here, :] = inv
            normed = (value * inv * gain[...]).astype(BF16)
            query = mm(normed, query_w[...])
            mixed = mm(normed, latent_w[...])
            latent = mixed[:, :R]

            @pl.when(g == 0)
            def _():
                latent_own[m] = latent[:tok]

            inv_l = lax.rsqrt(jnp.mean(latent * latent, axis=-1, keepdims=True) + EPS)
            low = (latent * inv_l * latent_gain[...]).astype(BF16)
            latent_n[m, here, :] = low
            q_nope[m, here, :] = query[:, :DN].astype(BF16)
            turned = query[:, DN:] * turn[here, :]
            q_rot[m, here, :] = (turned + pltpu.roll(turned, DR, 1)).astype(BF16)
            turned = mixed[:, R:] * turn[here, :]
            k_rot[m, here, :] = (turned + pltpu.roll(turned, DR, 1)).astype(BF16)
            kv = mm(low, expand_w[...])
            k_nope[m, here, :] = kv[:, :DN].astype(BF16)
            val[m, here, :] = kv[:, DN:].astype(BF16)

        if m + 1 < MICRO:
            for copy in loads[m + 1]:
                copy.start()
        half_k = jnp.where(lane < DR, k_rot[m], jnp.zeros_like(k_rot[m]))

        @pl.loop(0, 4)
        def _(g):
            here = pl.ds(pl.multiple_of(g * span, span), span)
            scores = mm_t(q_nope[m, here, :], k_nope[m]) + mm_t(q_rot[m, here, :], half_k)
            visible = (pos_k[...] <= pos_q[here, :]) & (pos_k[...] < length[m])
            scores = jnp.where(visible, scores * scale, -1e30)
            raised = jnp.exp(scores - jnp.max(scores, axis=-1, keepdims=True))
            prob = (raised / jnp.sum(raised, axis=-1, keepdims=True)).astype(BF16)
            probs[m, here, :] = prob
            value = mm(prob, val[m]).astype(BF16).reshape(quarter, tok, DV)
            for i in range(quarter):
                out[order[g * quarter + i], pl.ds(m * tok, tok), :] = value[i]


def attend(order, length, pieces, query_w, latent_w, expand_w, gain, latent_gain, turn, pos):
    blocks = sum(piece.shape[0] for piece in pieces)
    tok, width = pieces[0].shape[1] // MICRO, query_w.shape[0]
    seq = blocks * tok
    small = sds((MICRO, seq, 128))
    return call(
        attend_kernel,
        (sds((blocks, MICRO * tok, DV)), small, small, small, small, small,
         sds((MICRO, seq, R)), sds((MICRO, seq, seq)), sds((MICRO, seq, 1), F32),
         sds((MICRO, tok, R), F32)),
        [pltpu.SMEM] * 2 + [pl.ANY] * TREE + [pltpu.VMEM] * 8,
        [pltpu.VMEM((blocks, tok, width), BF16), pltpu.SemaphoreType.DMA((TREE,))],
        2 * MICRO * seq * (width * 896 + R * 256 + seq * 384),
        2 * MICRO * seq * (width + seq + 1200) + 1800 * width,
        order, length, *pieces, query_w, latent_w, expand_w, gain.reshape(1, -1),
        latent_gain.reshape(1, -1), turn, pos.reshape(seq, 1), pos.reshape(1, seq),
    )


def attend_back_kernel(order, *refs):
    pieces = refs[:TREE]
    (grad, q_nope, q_rot, k_nope, k_rot, val, latent_n, probs, factor, query_w, expand_w, gain,
     turn) = refs[TREE : TREE + 13]
    (grad_queries, l0, l1, l2, l3, l4, grad_query_w, grad_expand_w, part,
     x, prob_all, grad_k, grad_r, grad_v, sems, prob_sem) = refs[TREE + 13 :]
    blocks, tok, width = x.shape
    quarter = blocks // 4
    span = quarter * tok
    scale = (DN + DR) ** (-0.5)
    grad_query_w[...] = jnp.zeros_like(grad_query_w)
    part[...] = jnp.zeros_like(part)
    lane = lax.broadcasted_iota(jnp.int32, (1, 128), 1)
    for m in range(MICRO):
        load = pltpu.make_async_copy(probs.at[m], prob_all, prob_sem)
        run(tree_copies(pieces, x, sems, m) + [load])
        grad_k[...] = jnp.zeros_like(grad_k)
        grad_r[...] = jnp.zeros_like(grad_r)
        grad_v[...] = jnp.zeros_like(grad_v)

        @pl.loop(0, 4)
        def _(g):
            here = pl.ds(pl.multiple_of(g * span, span), span)
            above = jnp.concatenate(
                [grad[order[g * quarter + i], pl.ds(m * tok, tok), :] for i in range(quarter)],
                axis=0,
            )
            prob_low = prob_all[here, :]
            prob = prob_low.astype(F32)
            weighted = prob * mm_t(above, val[m])
            slope = (weighted - prob * jnp.sum(weighted, axis=-1, keepdims=True)).astype(BF16)
            grad_k[...] += t_mm(slope, q_nope[m, here, :])
            grad_r[...] += t_mm(slope, q_rot[m, here, :])
            grad_v[...] += t_mm(prob_low, above)
            nope = (mm(slope, k_nope[m]) * scale).astype(BF16)
            turned = mm(slope, k_rot[m]) * (scale * turn[here, :])
            grad_q = jnp.concatenate([nope, turned.astype(BF16)], axis=1)
            back = jnp.where(
                lane < DR // 2,
                turned + pltpu.roll(turned, DR // 2, 1),
                turned - pltpu.roll(turned, 128 - DR // 2, 1),
            )
            both = jnp.concatenate([nope, back.astype(BF16)], axis=1).reshape(quarter, tok, 256)
            for i in range(quarter):
                grad_queries[order[g * quarter + i], pl.ds(m * tok, tok), :] = both[i]
            value = rows_of(x, g * quarter, quarter).astype(F32) * factor[m, here, :]
            grad_query_w[...] += t_mm((value * gain[...]).astype(BF16), grad_q)
            normed = mm_t(grad_q, query_w[...])
            part[...] += jnp.sum(normed * value, axis=0, keepdims=True)

        grad_kv = jnp.concatenate([grad_k[...] * scale, grad_v[...]], axis=1).astype(BF16)
        expand_sum = t_mm(latent_n[m], grad_kv)
        grad_expand_w[...] = expand_sum if m == 0 else grad_expand_w[...] + expand_sum
        latent = jnp.concatenate(
            [mm_t(grad_kv, expand_w[...]).astype(BF16), (grad_r[...] * scale).astype(BF16)], axis=1
        ).reshape(blocks, tok, R + 128)
        at = 0
        for ref in (l0, l1, l2, l3, l4):
            count = ref.shape[0]
            ref[:, pl.ds(m * tok, tok), :] = latent[at : at + count]
            at += count


def attend_back(order, pieces, grad, saved, query_w, expand_w, gain, turn, marks):
    blocks = sum(piece.shape[0] for piece in pieces)
    both, width = pieces[0].shape[1], query_w.shape[0]
    tok = both // MICRO
    seq = blocks * tok
    quarter = blocks // 4
    sizes = (quarter,) * 3 + (quarter // 2,) * 2
    return call(
        attend_back_kernel,
        (sds((blocks, both, 256)),)
        + tuple(sds((count, both, R + 128)) for count in sizes)
        + (sds((width, 256), F32), sds((R, 256), F32), sds((1, width), F32)),
        [pltpu.SMEM] + [pl.ANY] * TREE + [pltpu.VMEM] * 7 + [pl.ANY] + [pltpu.VMEM] * 5,
        [pltpu.VMEM((blocks, tok, width), BF16), pltpu.VMEM((seq, seq), BF16)]
        + [pltpu.VMEM((seq, 128), F32)] * 3
        + [pltpu.SemaphoreType.DMA((TREE,)), pltpu.SemaphoreType.DMA],
        2 * MICRO * seq * (width * 512 + R * 512 + seq * 768),
        2 * MICRO * seq * (2 * width + seq + 2000) + 2 * query_w.size,
        order, *pieces, grad, *saved[1:9], query_w, expand_w, gain.reshape(1, -1), turn,
        marks=marks,
    )


def early_kernel(m, *refs):
    pieces = refs[:TREE]
    pick, row_gate, down, shared_down, back, grad_eh, grad_shared, whole, g, sems = refs[TREE:]
    blocks, tok, width = g.shape
    quarter = blocks // 4
    room = pick.shape[1]
    run(tree_copies(pieces, g, sems, m))

    @pl.loop(0, 4)
    def _(q):
        value = rows_of(g, q * quarter, quarter)
        here = pl.ds(pl.multiple_of(q * room, room), room)
        back[here, :] = (row_gate[here, :] * mm(pick[q], value)).astype(BF16)
        span = quarter * tok
        there = pl.ds(pl.multiple_of(q * span, span), span)
        grad_shared[there, :] = mm_t(value, shared_down[...])
        whole[there, :] = value

    chunks = down.shape[0] // 128

    @pl.loop(0, chunks)
    def _(f):
        here = pl.ds(pl.multiple_of(f * 128, 128), 128)
        grad_eh[:, here] = mm_t(back[...], down[here, :])


def early(m, pieces, pick, row_gate, down, shared_down, marks):
    blocks = sum(piece.shape[0] for piece in pieces)
    tok, width = pieces[0].shape[1] // MICRO, down.shape[1]
    rows, units = pick.shape[0] * pick.shape[1], shared_down.shape[0]
    return call(
        functools.partial(early_kernel, m),
        (sds((rows, width)), sds((rows, down.shape[0]), F32), sds((blocks * tok, units), F32),
         sds((blocks * tok, width))),
        [pl.ANY] * TREE + [pltpu.VMEM] * 4,
        [pltpu.VMEM((blocks, tok, width), BF16), pltpu.SemaphoreType.DMA((TREE,))],
        2 * rows * width * (down.shape[0] + 256),
        2 * width * (2 * blocks * tok + rows + down.shape[0]) + 4 * rows * down.shape[0],
        *pieces, pick, row_gate, down, shared_down, marks=marks,
    )


def expert_kernel(m, *refs):
    pieces = refs[:TREE]
    pick, grad_eh, grad_shared, both, share_g, share_u = refs[TREE : TREE + 6]
    first = TREE + 6 + (TREE if m else 0)
    mixed, arrived, hidden, grad_gu, shared_hidden, grad_sg, grad_su = refs[first : first + 7]
    outs = refs[first + 7 : first + 7 + TREE]
    x, w, o, sems, w_sems = refs[first + 7 + TREE :]
    blocks, tok, width = x.shape
    quarter = blocks // 4
    span = quarter * tok
    room = pick.shape[1]
    chunks = w.shape[0] // 256
    copies = tree_copies(pieces, x, sems, m)
    for copy in copies:
        copy.start()
    loads = [
        pltpu.make_async_copy(both.at[pl.ds(f * 256, 256)], w.at[pl.ds(f * 256, 256)], w_sems.at[f])
        for f in range(chunks)
    ]
    for copy in loads:
        copy.start()
    for copy in copies:
        copy.wait()

    @pl.loop(0, 4)
    def _(q):
        value = rows_of(x, q * quarter, quarter)
        there = pl.ds(pl.multiple_of(q * span, span), span)
        here = pl.ds(pl.multiple_of(q * room, room), room)
        mixed[there, :] = value
        arrived[here, :] = mm(pick[q], value).astype(BF16)
        gate = mm(value, share_g[...])
        lift = mm(value, share_u[...])
        sigma = 1.0 / (1.0 + jnp.exp(-gate))
        grad = grad_shared[there, :]
        shared_hidden[there, :] = (gate * sigma * lift).astype(BF16)
        grad_sg[there, :] = (grad * lift * sigma * (1.0 + gate * (1.0 - sigma))).astype(BF16)
        grad_su[there, :] = (grad * gate * sigma).astype(BF16)

    for copy in loads:
        copy.wait()

    @pl.loop(0, chunks)
    def _(f):
        rows = pl.ds(pl.multiple_of(f * 256, 256), 256)
        cols = pl.ds(pl.multiple_of(f * 128, 128), 128)
        value = mm_t(arrived[...], w[rows, :])
        gate, lift = value[:, :128], value[:, 128:]
        sigma = 1.0 / (1.0 + jnp.exp(-gate))
        grad = grad_eh[:, cols]
        hidden[:, cols] = (gate * sigma * lift).astype(BF16)
        grad_gu[:, rows] = jnp.concatenate(
            [
                (grad * lift * sigma * (1.0 + gate * (1.0 - sigma))).astype(BF16),
                (grad * gate * sigma).astype(BF16),
            ],
            axis=1,
        )

    spread_out(
        o, pick, 512,
        lambda cols: mm(grad_gu[...], w[:, cols]).astype(BF16),
        lambda there, cols: mm_t(grad_sg[there, :], share_g[cols, :])
        + mm_t(grad_su[there, :], share_u[cols, :]),
    )
    run(tree_copies(outs, o, sems, m, True))


def spread_out(o, pick, step, routed, shared):
    blocks, tok, width = o.shape
    quarter = blocks // 4
    span = quarter * tok
    room = pick.shape[1]

    @pl.loop(0, width // step)
    def _(c):
        cols = pl.ds(pl.multiple_of(c * step, step), step)
        value = routed(cols)
        for q in range(4):
            there = pl.ds(q * span, span)
            tokens = t_mm(pick[q], value[q * room : (q + 1) * room]) + shared(there, cols)
            o[pl.ds(q * quarter, quarter), :, cols] = tokens.astype(BF16).reshape(
                quarter, tok, step
            )


def experts(m, pieces, pick, grad_eh, grad_shared, both, share_g, share_u, earlier):
    blocks = sum(piece.shape[0] for piece in pieces)
    tok, width = pieces[0].shape[1] // MICRO, pieces[0].shape[2]
    seq, rows, units = blocks * tok, pick.shape[0] * pick.shape[1], share_g.shape[1]
    hid = both.shape[0] // 2
    whole = pltpu.VMEM((blocks, tok, width), BF16)
    return call(
        functools.partial(expert_kernel, m),
        (sds((seq, width)), sds((rows, width)), sds((rows, hid)), sds((rows, 2 * hid)))
        + (sds((seq, units)),) * 3 + tuple(sds(piece.shape) for piece in pieces),
        [pl.ANY] * TREE + [pltpu.VMEM] * 3 + [pl.ANY] + [pltpu.VMEM] * 2
        + [pl.ANY] * len(earlier),
        [whole, pltpu.VMEM(both.shape, BF16), whole,
         pltpu.SemaphoreType.DMA((TREE,)), pltpu.SemaphoreType.DMA((both.shape[0] // 256,))],
        8 * rows * width * hid + 8 * seq * width * 256,
        2 * both.size + 6 * seq * width + 10 * rows * hid,
        *pieces, pick, grad_eh, grad_shared, both, share_g, share_u, *earlier,
        outs=[pltpu.VMEM] * 7 + [pl.ANY] * TREE,
        aliases={TREE + 6 + i: 7 + i for i in range(len(earlier))},
    )


def output_kernel(m, *refs):
    hidden, row_gate, pick, down, shared_hidden, shared_down = refs[:6]
    first = 6 + (TREE if m else 0)
    outs = refs[first : first + TREE]
    o, sems = refs[first + TREE :]
    spread_out(
        o, pick, 512,
        lambda cols: (
            row_gate[...] * mm(hidden[...], down[:, cols]).astype(BF16).astype(F32)
        ).astype(BF16),
        lambda there, cols: mm(shared_hidden[there, :], shared_down[:, cols]),
    )
    run(tree_copies(outs, o, sems, m, True))


def expert_output(m, pieces, hidden, row_gate, pick, down, shared_hidden, shared_down, earlier,
                  marks):
    blocks = sum(piece.shape[0] for piece in pieces)
    tok, width = pieces[0].shape[1] // MICRO, pieces[0].shape[2]
    return call(
        functools.partial(output_kernel, m),
        tuple(sds(piece.shape) for piece in pieces),
        [pltpu.VMEM] * 6 + [pl.ANY] * len(earlier),
        [pltpu.VMEM((blocks, tok, width), BF16), pltpu.SemaphoreType.DMA((TREE,))],
        2 * hidden.size * width + 4 * blocks * tok * 256 * width,
        2 * down.size + 2 * hidden.size + 2 * blocks * tok * width,
        hidden, row_gate, pick, down, shared_hidden, shared_down, *earlier,
        marks=marks,
        outs=[pl.ANY] * TREE,
        aliases={6 + i: i for i in range(len(earlier))},
    )


def weight_kernel(reps, count, *refs):
    l0, l1, r0, r1, *outs = refs[count:]
    unit = 128 // reps
    value = t_mm(l0[...], r0[...]) + t_mm(l1[...], r1[...])
    for index, ref in enumerate(outs):
        for part in range(reps):
            start = index * 128 + part * unit
            ref[part] = value[start : start + unit].astype(ref.dtype)


def weight_sums(reps, lanes, left, right, marks):
    rows, width = right[0].shape
    hid = left[0].shape[1] * 128 // lanes
    chunks, unit = hid // 128, 128 // reps
    whole = pl.BlockSpec((rows, width), lambda f: (0, 0), pipeline_mode=pl.Buffered(1))
    part = pl.BlockSpec((reps, unit, width), lambda f: (0, f, 0))
    return pl.pallas_call(
        functools.partial(weight_kernel, reps, len(marks)),
        grid=(chunks,),
        in_specs=[pl.BlockSpec(memory_space=pl.ANY)] * len(marks)
        + [pl.BlockSpec((rows, lanes), lambda f: (0, f))] * 2 + [whole] * 2,
        out_specs=[part] * (lanes // 128),
        out_shape=[sds((reps, hid // reps, width))] * (lanes // 128),
        compiler_params=pltpu.CompilerParams(vmem_limit_bytes=LIMIT),
        cost_estimate=pl.CostEstimate(
            flops=4 * rows * width * hid * lanes // 128,
            bytes_accessed=10 * width * hid,
            transcendentals=0,
        ),
    )(*marks, *left, *right)


def rep_pull(value, count, step):
    return lax.ppermute(value, "rep", [((d + step) % count, d) for d in range(count)])


def rep_parts(value, count):
    return [value] + [rep_pull(value, count, step) for step in range(1, count)]


def rep_total(parts, count):
    value = parts[0].astype(F32)
    for step in range(1, count):
        perm = [(d, (d + step) % count) for d in range(count)]
        value = value + lax.ppermute(parts[step], "rep", perm).astype(F32)
    return value


def rep_sum(value):
    return jnp.sum(lax.all_gather(value.astype(BF16), "rep", axis=0).astype(F32), axis=0)


def body(
    hidden_in,
    cotangent,
    lengths,
    routes,
    gate_values,
    attn_gain,
    query_proj,
    latent_proj,
    latent_gain,
    expand_proj,
    output_proj,
    ffn_gain,
    shared_gate,
    shared_lift,
    shared_down,
    expert_gate,
    expert_lift,
    expert_down,
):
    tok = hidden_in.shape[1]
    width = hidden_in.shape[2]
    n = lax.axis_size("fsdp")
    reps = lax.axis_size("rep")
    me = lax.axis_index("fsdp")
    rep = lax.axis_index("rep")
    outer = n // 4
    seq = tok * n
    capacity = min(tok, 3 * tok * TOP // (2 * n))
    split = max(1, n // H)
    rows = width // n

    slots = jnp.arange(n, dtype=jnp.int32)
    nearness = near_first(outer)
    steps_on = jnp.asarray(nearness, jnp.int32)
    place_of = jnp.asarray([nearness.index(k) for k in range(outer)], jnp.int32)
    abs_of_rel = ((me // 4 + steps_on[slots % outer]) % outer) * 4 + ((me % 4) ^ (slots // outer))
    rel_of_abs = ((slots % 4) ^ (me % 4)) * outer + place_of[(slots // 4 - me // 4) % outer]
    rep_order = (jnp.arange(reps, dtype=jnp.int32) - rep) % reps
    own_pos = me * tok + jnp.arange(tok, dtype=jnp.int32)
    pos = (abs_of_rel[:, None] * tok + jnp.arange(tok, dtype=jnp.int32)[None, :]).reshape(seq)
    freqs = THETA ** (-(2.0 * jnp.arange(DR // 2, dtype=F32)) / DR)
    angles = pos.astype(F32)[:, None] * freqs[None, :]
    cosine, sine = jnp.cos(angles), jnp.sin(angles)
    turn = jnp.concatenate([cosine, cosine, sine, sine], axis=1)

    def all_to_all(value):
        return lax.all_to_all(value, "fsdp", split_axis=0, concat_axis=0, tiled=True)

    def rep_slice(value, axis):
        size = value.shape[axis] // reps
        return lax.dynamic_slice_in_dim(value, rep * size, size, axis)

    def rep_join(value, axis):
        parts = jnp.take(jnp.stack(rep_parts(value, reps)), rep_order, axis=0)
        return jnp.concatenate([parts[i] for i in range(reps)], axis=axis)

    def unreshard(value):
        return rep_sum(all_to_all(value.astype(BF16)))

    def by_head(value):
        return jnp.repeat(value, split, axis=0) if split > 1 else value

    both = MICRO * tok
    dense_gate = jnp.sum(
        jnp.where(routes[..., None] == slots, gate_values[..., None], 0.0), axis=2
    ).reshape(both, n)
    gate_high = dense_gate.astype(BF16)
    gate_low = (dense_gate - gate_high.astype(F32)).astype(BF16)

    def fit(value):
        return jnp.pad(value, ((0, both - value.shape[0]), (0, 0)))

    items = [
        fit(latent_proj),
        gate_high,
        gate_low,
        fit(attn_gain[:, None]),
        fit(ffn_gain[:, None]),
        fit(latent_gain[:, None]),
    ]
    starts = [0]
    for item in items:
        starts.append(starts[-1] + item.shape[1])
    fill = jnp.zeros((both, -starts[-1] % 128), BF16)
    small = gather_small("small", jnp.concatenate(items + [fill], axis=1), n)[0]
    extras = jnp.concatenate(small, axis=0)
    latent_w = jnp.take(extras[:, :rows, : starts[1]], rel_of_abs, axis=0).reshape(width, R + DR)
    gates = extras[..., starts[1] : starts[3]].reshape(n, both, 2, n).astype(F32)
    gates = jnp.sum(jnp.where(slots == me, gates, 0.0), axis=(2, 3))
    gains = jnp.take(extras[..., starts[3] : starts[6]], rel_of_abs, axis=0).astype(F32)
    gains = jnp.transpose(gains, (2, 0, 1))
    attn_gain_f = gains[0, :, :rows].reshape(width)
    ffn_gain_f = gains[1, :, :rows].reshape(width)
    latent_gain_f = gains[2, :, : R // n].reshape(R)

    head_w = jnp.concatenate(
        [
            jnp.transpose(query_proj.reshape(rows, H, DN + DR), (1, 0, 2)),
            jnp.transpose(expand_proj.reshape(R // n, H, DN + DV), (1, 0, 2)).reshape(
                H, rows, -1
            ),
        ],
        axis=2,
    )
    head_w = all_to_all(by_head(head_w))
    query_w = head_w[..., : DN + DR].reshape(width, DN + DR)
    expand_w = head_w[..., DN + DR :].reshape(R, DN + DV)
    query_w = jnp.concatenate([query_w] + swapped(query_w[:, DN:]), axis=1)
    latent_in = jnp.concatenate([latent_w] + swapped(latent_w[:, R:]), axis=1)

    unit = 128 // reps

    def chunked(*weights):
        parts = [lax.all_gather(item, "rep", axis=0) for item in weights]
        return jnp.stack(
            [part[i].reshape(-1, unit, width) for part in parts for i in range(reps)], axis=1
        ).reshape(-1, width)

    both_w = chunked(jnp.swapaxes(expert_gate[0], 0, 1), jnp.swapaxes(expert_lift[0], 0, 1))
    down_w = chunked(expert_down[0])
    block = hidden_in.reshape(both, width)
    hidden_all, given = gather_tree(
        "hidden", block, n, ((), (), [query_w, latent_in, expand_w, both_w, down_w])
    )
    query_w, latent_in, expand_w, both_w, down_w = given[2]

    cols = width // reps
    used = (own_pos[None, :] < lengths[:, None])[..., None]
    grad_rows = jnp.where(used, cotangent, jnp.zeros_like(cotangent)).reshape(both, width)
    (out_share,), hidden_all[1:2] = order_after([rep_slice(output_proj, 1)], hidden_all[1:2])
    out_marks = hidden_all[3:4]
    att = attend(
        abs_of_rel, lengths, hidden_all, query_w, latent_in, expand_w,
        attn_gain_f, latent_gain_f, turn, pos,
    )
    att = list(att)

    out_pieces, _, att[0:1] = gather_small("output_w", out_share, n, out_marks, att[0:1])
    heads_out = all_to_all(att[0])
    (grad_rows,), out_pieces[0:1] = order_after([grad_rows], out_pieces[0:1])
    grad_all, given = gather_tree("cotangent", grad_rows, n, (out_pieces[1:3] + [heads_out], (), ()))
    out_pieces[1], out_pieces[2], heads_out = given[0]
    heads_out = heads_out[::split]
    heads_local = jnp.transpose(heads_out, (1, 0, 2)).reshape(both, n, H * DV // n)
    heads_local = jnp.take(heads_local, abs_of_rel, axis=1).reshape(both, H * DV)
    cols = width // reps
    out_w = rep_parts(jnp.concatenate(out_pieces, axis=0).reshape(H * DV, cols), reps)

    def columns(step):
        return ((rep + step) % reps) * cols

    merge = 1
    while (merge * capacity) % 16:
        merge *= 2
    groups = n // merge
    span = merge * tok
    room = merge * capacity
    upper = (jnp.arange(span)[:, None] <= jnp.arange(span)[None, :]).astype(BF16)

    hidden = hidden_in.reshape(both, width).astype(F32)
    residual = jnp.zeros((both, width), F32)
    for step in range(reps):
        share = contract("tj,jd->td", heads_local, out_w[step])
        residual = lax.dynamic_update_slice(residual, share, (0, columns(step)))
    residual = hidden + residual
    mixed, inv_second = rms_forward(residual, ffn_gain_f)
    mixed = mixed.astype(BF16)
    (shared_gate, shared_lift), (mixed,) = order_after([shared_gate, shared_lift], [mixed])

    ahead = []
    for m in range(MICRO):
        gate_here = gates[:, m * tok : (m + 1) * tok].reshape(groups, span)
        hit = gate_here > 0.0
        place = contract("gt,ts->gs", hit.astype(BF16), upper).astype(jnp.int32) - 1
        chosen = hit[:, None, :] & (
            place[:, None, :] == jnp.arange(room, dtype=jnp.int32)[None, :, None]
        )
        pick = chosen.astype(BF16)
        row_gate = jnp.sum(jnp.where(chosen, gate_here[:, None, :], 0.0), axis=2).reshape(-1, 1)
        ahead.append(
            (pick, row_gate) + early(m, grad_all, pick, row_gate, down_w, shared_down,
                    (ahead[0][2],) if m else (mixed,))
        )

    shared_in = jnp.concatenate(
        [
            jnp.transpose(shared_gate.reshape(rows, n, -1), (1, 0, 2)),
            jnp.transpose(shared_lift.reshape(rows, n, -1), (1, 0, 2)),
        ],
        axis=2,
    )
    units = shared_in.shape[2] // 2
    shared_in = all_to_all(shared_in)
    marks = [list(item) for item in ahead]
    mixed_all, given = gather_tree(
        "mixed", mixed, n, ((), [marks[0][2], shared_in, both_w], [marks[1][2]])
    )
    marks[0][2], shared_in, both_w = given[1]
    marks[1][2:3] = given[2]
    shared_in = shared_in.reshape(width, 2 * units)
    ahead = marks

    share_g, share_u = shared_in[:, :units], shared_in[:, units:]

    share = jnp.concatenate([rep_slice(query_proj, 1)], axis=1)
    (share,), mixed_all[8:] = order_after([share], mixed_all[8:])
    whole_query = lax.all_gather(share, "fsdp", axis=0, tiled=True)

    done = []
    earlier = ()
    for m in range(MICRO):
        pick, row_gate, back, grad_eh, grad_shared, _ = ahead[m]
        done.append(
            experts(m, mixed_all, pick, grad_eh, grad_shared, both_w, share_g, share_u, earlier)
        )
        earlier = done[m][7:]
    earlier = list(earlier)
    pieces = ()
    halves = scatter_tree_last("grad_mixed", earlier, n)
    bases = scatter_tree_cross("grad_mixed", halves, n)
    stages = [(halves[0][1],), (halves[1][2],), (bases[0][0],), (bases[1][0],)]
    for m in range(MICRO):
        pick, row_gate = ahead[m][:2]
        pieces = list(
            expert_output(
                m, mixed_all, done[m][2], row_gate, pick, down_w, done[m][4], shared_down,
                pieces, stages[2 * m],
            )
        )
        if m == 0:
            down_sums = list(
                weight_sums(
                    reps, 128, (done[0][2], done[1][2]), (ahead[0][2], ahead[1][2]),
                    stages[1] + (pieces[0],),
                )
            )
            share_grads, down_sums[0:1] = order_after(
                [done[0][5], done[1][5]], list(down_sums[0:1])
            )
            stages[2] += (down_sums[0],)
    down_sums = list(down_sums)
    both_sums = weight_sums(
        reps, 256, (done[0][3], done[1][3]), (done[0][1], done[1][1]),
        stages[3] + (pieces[0],),
    )
    both_sums = list(both_sums)
    grad_mixed, _ = scatter_tree_rest("grad_mixed", bases, n)
    grad_shared_in = sum(
        contract("td,tf->df", done[m][0], jnp.concatenate([share_grads[m], done[m][6]], axis=1))
        for m in range(MICRO)
    )
    grad_shared_in = all_to_all(grad_shared_in.astype(BF16).reshape(n, rows, 2 * units))
    halves = [list(item) for item in scatter_tree_last("routed", pieces, n)]
    (grad_mixed,), given = order_after(
        [grad_mixed], [both_sums[0], grad_shared_in] + halves[0][1:] + halves[1][1:]
    )
    both_sums[0], grad_shared_in = given[:2]
    halves[0][1:], halves[1][1:] = given[2:4], given[4:]
    whole_query = lax.all_gather(whole_query, "rep", axis=0)
    expert_sums = [
        lax.psum_scatter(item, "rep", scatter_dimension=0) for item in both_sums + down_sums
    ]
    grad_res, part_ffn = rms_backward(residual, inv_second, ffn_gain_f, grad_mixed)
    grad_res = grad_res + grad_rows.astype(F32)
    grad_res_low = grad_res.astype(BF16)
    grad_heads = sum(
        contract(
            "td,jd->tj",
            lax.dynamic_slice_in_dim(grad_res_low, columns(step), cols, 1),
            out_w[step],
        )
        for step in range(reps)
    )
    grad_heads = jnp.take(
        grad_heads.astype(BF16).reshape(both, n, H * DV // n), rel_of_abs, axis=1
    )
    grad_heads = jnp.transpose(grad_heads.reshape(both, H, DV), (1, 0, 2))
    grad_heads = by_head(grad_heads)
    grad_heads = all_to_all(grad_heads)
    if split > 1:
        grad_heads = jnp.where(me % split == 0, grad_heads, jnp.zeros_like(grad_heads))

    shares = []
    for step in range(reps):
        piece = lax.dynamic_slice_in_dim(grad_res_low, columns(step), cols, 1)
        shares.append(contract("tj,td->jd", heads_local, piece))
    out_total = rep_total([shares[0]] + [item.astype(BF16) for item in shares[1:]], reps)
    out_total = out_total.astype(BF16).reshape(n, rows, cols)
    out_pieces = small_split(out_total)

    result = attend_back(
        abs_of_rel, hidden_all, grad_heads, att, query_w, expand_w, attn_gain_f, turn,
        [whole_query] + expert_sums,
    )
    result = list(result)
    expert_sums, result[1:2] = order_after(expert_sums, result[1:2])
    grad_expert_gate, grad_expert_lift, grad_expert_down = [
        item.astype(F32) for item in expert_sums
    ]
    (grad_shared_in,), result[2:3] = order_after([grad_shared_in], result[2:3])
    grad_shared_in = rep_sum(grad_shared_in)
    grad_shared_gate = jnp.transpose(grad_shared_in[:, :, :units], (1, 0, 2)).reshape(rows, -1)
    grad_shared_lift = jnp.transpose(grad_shared_in[:, :, units:], (1, 0, 2)).reshape(rows, -1)
    down_sum = sum(contract("tf,td->fd", done[m][4], ahead[m][5]) for m in range(MICRO))
    grad_shared_down = rep_sum(down_sum)


    bases = scatter_tree_cross("routed", halves, n)
    bases, result[6:7] = order_bases(bases, result[6:7])
    grad_queries = all_to_all(result[0])
    grad_latent = scatter_small_last("grad_latent", result[1:6], n)
    grad_latent, (grad_queries,) = scatter_small_rest(
        "grad_latent", grad_latent, n, [grad_queries]
    )
    routed, (grad_latent,) = scatter_tree_rest("routed", bases, n, [grad_latent])
    outputs = (residual + routed).astype(BF16).reshape(MICRO, tok, width)
    out_pieces[3:], (grad_latent,) = order_after(out_pieces[3:], [grad_latent])
    out_pieces = scatter_small_last("grad_output_w", out_pieces, n)
    grad_q, grad_expand_w, part_attn = result[6:]

    latent = att[9].reshape(both, R)
    inv = lax.rsqrt(jnp.mean(latent * latent, axis=-1, keepdims=True) + EPS)
    grad_c, part_latent = rms_backward(latent, inv, latent_gain_f, grad_latent[:, :R])
    own_cos, own_sin = jnp.tile(cosine[:tok], (MICRO, 1)), jnp.tile(sine[:tok], (MICRO, 1))
    grad_krope = rotate_back(grad_latent[:, R : R + DR], own_cos, own_sin)
    grad_kva = jnp.concatenate([grad_c, grad_krope], axis=1).astype(BF16)
    grad_local = contract("tj,dj->td", grad_kva, latent_w)
    factor = att[8][:, :tok].reshape(both, 1)
    part_attn = part_attn[0] + jnp.sum(grad_local * hidden * factor, axis=0)

    gain_parts = jnp.stack(
        [
            part_attn.reshape(n, rows),
            part_ffn.reshape(n, rows),
            jnp.pad(part_latent.reshape(n, R // n), ((0, 0), (0, rows - R // n))),
        ],
        axis=1,
    )
    kv_pieces = gather_small("grad_kv", grad_kva, n)[0]

    turn_part = grad_q[:, DN + DR :]
    half = DR // 2
    grad_q = jnp.concatenate(
        [
            grad_q[:, :DN],
            grad_q[:, DN : DN + half] + turn_part[:, half:],
            grad_q[:, DN + half : DN + DR] - turn_part[:, :half],
        ],
        axis=1,
    )
    head_grad = jnp.concatenate(
        [grad_q.reshape(n, rows, DN + DR), grad_expand_w.reshape(n, rows, -1)], axis=2
    ).astype(BF16)
    gain_high = gain_parts.astype(BF16)
    gain_low = (gain_parts - gain_high.astype(F32)).astype(BF16)
    gain_rows = jnp.stack([gain_high, gain_low], axis=1).reshape(n, -1)
    gain_count = gain_rows.shape[1]
    head_cols = head_grad.shape[2]
    gain_rows = jnp.pad(gain_rows, ((0, 0), (0, 16 * head_cols - gain_count)))
    head_grad = jnp.concatenate([head_grad, gain_rows.reshape(n, 16, head_cols)], axis=1)
    (head_grad,), (grad_queries,) = order_after([head_grad], [grad_queries])
    head_grad = all_to_all(head_grad)
    gain_sum = head_grad[:, rows:].reshape(n, -1)[:, :gain_count].astype(F32)
    gain_sum = jnp.sum(gain_sum, axis=0).reshape(2, 3, rows)
    gain_sum = gain_sum[0] + gain_sum[1]
    head_grad = head_grad[:, :rows]
    out_sum, kv_pieces[3:] = scatter_small_rest("grad_output_w", out_pieces, n, kv_pieces[3:])
    (head_grad,), (out_sum,) = order_after([head_grad], [out_sum])
    head_grad = rep_sum(head_grad)[::split]
    grad_output_proj = rep_join(out_sum.astype(BF16), 1).astype(F32)
    grad_queries = jnp.transpose(grad_queries[::split, :, : DN + DR], (1, 0, 2))
    grad_queries = grad_queries.reshape(both, reps, -1)
    grad_normed = sum(
        contract("tj,dj->td", grad_queries[:, i], whole_query[i]) for i in range(reps)
    )
    grad_first, _ = rms_backward(hidden, factor, attn_gain_f, grad_normed + grad_local)
    input_grads = (grad_first + grad_res).astype(BF16).reshape(MICRO, tok, width)

    grad_query_proj = jnp.transpose(head_grad[..., : DN + DR], (1, 0, 2)).reshape(rows, -1)
    grad_expand_proj = jnp.transpose(
        head_grad[..., DN + DR :].reshape(H, R // n, DN + DV), (1, 0, 2)
    ).reshape(R // n, H * (DN + DV))

    kv_blocks = jnp.concatenate(kv_pieces, axis=0)
    hidden_all, (grad_queries,) = order_after(hidden_all, [grad_queries])
    gain_cols = lax.dynamic_slice_in_dim(attn_gain_f, me * rows, rows, 0)
    hidden_cols = jnp.concatenate(
        [lax.dynamic_slice_in_dim(item, me * rows, rows, 2) for item in hidden_all], axis=0
    ).reshape(n, MICRO, tok, rows)
    factors = jnp.swapaxes(att[8].reshape(MICRO, n, tok, 1), 0, 1)
    normed_cols = (hidden_cols.astype(F32) * factors * gain_cols).astype(BF16)
    latent_total = contract(
        "tj,td->jd", kv_blocks.reshape(-1, R + DR), normed_cols.reshape(-1, rows)
    )
    latent_total = rep_sum(latent_total)
    grad_latent_proj = latent_total.T

    gain_sum = gain_sum + sum(rep_pull(gain_sum, reps, step) for step in range(1, reps))

    return (
        outputs,
        input_grads,
        gain_sum[0],
        grad_query_proj,
        grad_latent_proj,
        gain_sum[2, : R // n],
        grad_expand_proj,
        grad_output_proj,
        gain_sum[1],
        grad_shared_gate,
        grad_shared_lift,
        grad_shared_down,
        jnp.swapaxes(grad_expert_gate, 0, 1)[None],
        jnp.swapaxes(grad_expert_lift, 0, 1)[None],
        grad_expert_down[None],
    )


def solution(mesh):
    in_specs = (
        P("rep", "fsdp", None),
        P("rep", "fsdp", None),
        P("rep"),
        P("rep", "fsdp", None),
        P("rep", "fsdp", None),
        P("fsdp"),
        P("fsdp", None),
        P("fsdp", None),
        P("fsdp"),
        P("fsdp", None),
        P("fsdp", None),
        P("fsdp"),
        P("fsdp", None),
        P("fsdp", None),
        P("fsdp", None),
        P("fsdp", None, "rep"),
        P("fsdp", None, "rep"),
        P("fsdp", "rep", None),
    )
    out_specs = (
        P("rep", "fsdp", None),
        P("rep", "fsdp", None),
        P("fsdp"),
        P("fsdp", None),
        P("fsdp", None),
        P("fsdp"),
        P("fsdp", None),
        P("fsdp", None),
        P("fsdp"),
        P("fsdp", None),
        P("fsdp", None),
        P("fsdp", None),
        P("fsdp", None, "rep"),
        P("fsdp", None, "rep"),
        P("fsdp", "rep", None),
    )
    return jax.shard_map(body, mesh=mesh, in_specs=in_specs, out_specs=out_specs, check_vma=False)
```

```python
import functools

import jax
import jax.numpy as jnp
from jax import lax
from jax.experimental import pallas as pl
from jax.experimental.pallas import tpu as pltpu
from jax.sharding import PartitionSpec as P

H = 16
DN = 128
DR = 64
DV = 128
R = 512
TOP = 6
MICRO = 2

EPS = 1e-06
THETA = 10000.0
F32 = jnp.float32
BF16 = jnp.bfloat16


def contract(form, left, right):
    return jnp.einsum(form, left, right, preferred_element_type=F32)


def rms_forward(value, gain):
    factor = lax.rsqrt(jnp.mean(value * value, axis=-1, keepdims=True) + EPS)
    return (value * factor * gain, factor)


def rms_backward(value, factor, gain, grad):
    scaled = grad * gain
    inner = jnp.mean(value * scaled, axis=-1, keepdims=True)
    return (
        factor * scaled - value * factor * factor * factor * inner,
        jnp.sum(grad * value * factor, axis=0),
    )


def rotate_back(grad, cosine, sine):
    half = grad.shape[-1] // 2
    first = grad[..., :half]
    second = grad[..., half:]
    return jnp.concatenate(
        [first * cosine + second * sine, second * cosine - first * sine], axis=-1
    )


def swapped(weight):
    half = weight.shape[1] // 2
    return [-weight[:, half:], weight[:, :half]]


def named(function):
    def scoped(name, *args):
        with jax.named_scope(name):
            return function(*args)

    return scoped


def near_first(outer):
    return [0] + [k for _, k in sorted((min(k, outer - k), k) for k in range(1, outer))]


def partners(devices, q, k):
    outer = devices // 4
    return [(d, ((d // 4 + k) % outer) * 4 + ((d % 4) ^ q)) for d in range(devices)]


def pull(value, devices, q, k=0):
    perm = [(there, here) for here, there in partners(devices, q, k)]
    return lax.ppermute(value, "fsdp", perm)


def push(value, devices, q, k=0):
    return lax.ppermute(value, "fsdp", partners(devices, q, k))


def order_after(values, marks):
    values, marks = list(values), list(marks)
    if not marks:
        return values, marks
    both = lax.optimization_barrier(tuple(values + marks))
    return list(both[: len(values)]), list(both[len(values) :])


def total(first, *others):
    value = first.astype(F32)
    for item in others:
        value = value + item.astype(F32)
    return value


@named
def gather_small(block, devices, cross_marks=(), last_marks=()):
    outer = devices // 4
    half = outer // 2
    base = jnp.stack([block] + [pull(block, devices, 0, k) for k in near_first(outer)[1:]])
    (sent,), cross_marks = order_after([base], cross_marks)
    one = pull(sent, devices, 1)
    two = pull(sent, devices, 2)
    (low, high), last_marks = order_after([one[:half], two[half:]], last_marks)
    low, high = pull(low, devices, 2), pull(high, devices, 1)
    return [base, one, two, low, high], cross_marks, last_marks


@named
def scatter_small_last(pieces, devices):
    base, one, two, low, high = pieces
    half = devices // 8
    low = push(low, devices, 2)
    high = push(high, devices, 1)
    zero = (0,) * one.ndim
    one = lax.dynamic_update_slice(one, total(one[:half], low).astype(BF16), zero)
    two = lax.dynamic_update_slice(
        two, total(two[half:], high).astype(BF16), (half,) + zero[1:]
    )
    return base, one, two


@named
def scatter_small_rest(pieces, devices, marks=()):
    base, one, two = pieces
    outer = devices // 4
    base = total(base, push(one, devices, 1), push(two, devices, 2))
    (sent,), marks = order_after([base[1:].astype(BF16)], marks)
    order = near_first(outer)
    return total(
        base[0], *[push(sent[i - 1], devices, 0, order[i]) for i in range(1, outer)]
    ), marks


@named
def gather_tree(block, devices, marks):
    outer = devices // 4
    half, part = outer // 2, outer // 4
    marks = [list(items) for items in marks]
    held = [block]
    for k in near_first(outer)[1:]:
        held.append(pull(block, devices, 0, k))
    pieces = [[], [], [], []]
    before = []
    for place, base in enumerate((held[:half], held[half:])):
        base = jnp.stack(base)
        if place == 0:
            (base,), marks[0] = order_after([base], marks[0])
        else:
            (base,), given = order_after([base], before + marks[1])
            pieces[1], pieces[2], marks[1] = given[0:1], given[1:2], given[2:]
        one = pull(base, devices, 1)
        two = pull(base, devices, 2)
        before = [one, two]
        low, high = one[:part], two[part:]
        if place:
            (low, high), given = order_after([low, high], pieces[3] + marks[2])
            pieces[3], marks[2] = given[:2], given[2:]
        last = [pull(low, devices, 2), pull(high, devices, 1)]
        for q, items in enumerate(([base], [one], [two], last)):
            pieces[q] += items
    return sum(pieces, []), marks


@named
def scatter_tree_last(pieces, devices):
    part = devices // 16
    halves = []
    for here in (1, 0):
        base, one, two = pieces[here], pieces[2 + here], pieces[4 + here]
        low, high = pieces[6 + 2 * here : 8 + 2 * here]
        low = push(low, devices, 2)
        high = push(high, devices, 1)
        zero = (0,) * one.ndim
        one = lax.dynamic_update_slice(one, total(one[:part], low).astype(BF16), zero)
        two = lax.dynamic_update_slice(
            two, total(two[part:], high).astype(BF16), (part,) + zero[1:]
        )
        halves.append((base, one, two))
    return halves


@named
def scatter_tree_cross(halves, devices):
    bases = []
    for base, one, two in halves:
        one = push(one, devices, 1)
        two = push(two, devices, 2)
        bases.append([total(base[i], one[i], two[i]) for i in range(base.shape[0])])
    return bases


@named
def scatter_tree_rest(bases, devices, marks=()):
    outer = devices // 4
    order = near_first(outer)
    sent, marks = order_after(
        [item.astype(BF16) for item in bases[0] + bases[1][1:]], marks
    )
    steps = order[outer // 2 :] + order[1 : outer // 2]
    arrived = [push(item, devices, 0, k) for item, k in zip(sent, steps)]
    return total(bases[1][0], *arrived), marks


def order_bases(bases, marks):
    values, marks = order_after(bases[0] + bases[1], marks)
    half = len(bases[0])
    return [values[:half], values[half:]], marks


def tree_sizes(devices):
    outer = devices // 4
    return [outer // 2] * 6 + [outer // 4] * 4


def small_split(value):
    count = value.shape[0] // 4
    half = count // 2
    cuts = (0, count, 2 * count, 3 * count, 3 * count + half, 4 * count)
    return [value[a:b] for a, b in zip(cuts, cuts[1:])]


LIMIT = 58 * 1024 * 1024


def mm(left, right):
    return jnp.dot(left, right, preferred_element_type=F32)


def mm_t(left, right):
    return lax.dot_general(left, right, (((1,), (1,)), ((), ())), preferred_element_type=F32)


def t_mm(left, right):
    return lax.dot_general(left, right, (((0,), (0,)), ((), ())), preferred_element_type=F32)


TREE = 10


def call(kernel, out_shape, places, scratch, flops, moved, *args, outs=None, aliases=None, marks=()):
    count = len(args)

    def without_marks(*refs):
        kernel(*refs[:count], *refs[count + len(marks) :])

    outs = outs or [pltpu.VMEM] * len(out_shape)
    places = list(places) + [pl.ANY] * len(marks)
    return pl.pallas_call(
        without_marks,
        out_shape=out_shape,
        in_specs=[pl.BlockSpec(memory_space=place) for place in places],
        out_specs=tuple(pl.BlockSpec(memory_space=place) for place in outs),
        input_output_aliases=aliases or {},
        scratch_shapes=scratch,
        compiler_params=pltpu.CompilerParams(vmem_limit_bytes=LIMIT),
        cost_estimate=pl.CostEstimate(flops=flops, bytes_accessed=moved, transcendentals=0),
    )(*args, *marks)


def sds(shape, dtype=BF16):
    return jax.ShapeDtypeStruct(shape, dtype)


def tree_copies(pieces, whole, sems, m, out=False):
    tok = whole.shape[1]
    copies, at = [], 0
    for place, piece in enumerate(pieces):
        count = piece.shape[0]
        ends = piece.at[:, pl.ds(m * tok, tok)], whole.at[pl.ds(at, count)]
        if out:
            ends = ends[::-1]
        copies.append(pltpu.make_async_copy(*ends, sems.at[place]))
        at += count
    return copies


def run(copies):
    for copy in copies:
        copy.start()
    for copy in copies:
        copy.wait()


def rows_of(whole, start, count):
    value = whole[pl.ds(start, count)]
    return value.reshape(count * value.shape[1], value.shape[2])


def attend_kernel(
    order, length, *refs,
):
    pieces = refs[:TREE]
    (query_w, latent_w, expand_w, gain, latent_gain, turn, pos_q, pos_k,
     out, q_nope, q_rot, k_nope, k_rot, val, latent_n, probs, factor, latent_own,
     x, sems) = refs[TREE:]
    blocks, tok, width = x.shape
    quarter = blocks // 4
    span = quarter * tok
    scale = (DN + DR) ** (-0.5)
    lane = lax.broadcasted_iota(jnp.int32, (1, 128), 1)
    loads = [tree_copies(pieces, x, sems, m) for m in range(MICRO)]
    for copy in loads[0]:
        copy.start()
    for m in range(MICRO):
        for copy in loads[m]:
            copy.wait()

        @pl.loop(0, 4)
        def _(g):
            here = pl.ds(pl.multiple_of(g * span, span), span)
            value = rows_of(x, g * quarter, quarter).astype(F32)
            inv = lax.rsqrt(jnp.mean(value * value, axis=-1, keepdims=True) + EPS)
            factor[m, here, :] = inv
            normed = (value * inv * gain[...]).astype(BF16)
            query = mm(normed, query_w[...])
            mixed = mm(normed, latent_w[...])
            latent = mixed[:, :R]

            @pl.when(g == 0)
            def _():
                latent_own[m] = latent[:tok]

            inv_l = lax.rsqrt(jnp.mean(latent * latent, axis=-1, keepdims=True) + EPS)
            low = (latent * inv_l * latent_gain[...]).astype(BF16)
            latent_n[m, here, :] = low
            q_nope[m, here, :] = query[:, :DN].astype(BF16)
            turned = query[:, DN:] * turn[here, :]
            q_rot[m, here, :] = (turned + pltpu.roll(turned, DR, 1)).astype(BF16)
            turned = mixed[:, R:] * turn[here, :]
            k_rot[m, here, :] = (turned + pltpu.roll(turned, DR, 1)).astype(BF16)
            kv = mm(low, expand_w[...])
            k_nope[m, here, :] = kv[:, :DN].astype(BF16)
            val[m, here, :] = kv[:, DN:].astype(BF16)

        if m + 1 < MICRO:
            for copy in loads[m + 1]:
                copy.start()
        half_k = jnp.where(lane < DR, k_rot[m], jnp.zeros_like(k_rot[m]))

        @pl.loop(0, 4)
        def _(g):
            here = pl.ds(pl.multiple_of(g * span, span), span)
            scores = mm_t(q_nope[m, here, :], k_nope[m]) + mm_t(q_rot[m, here, :], half_k)
            visible = (pos_k[...] <= pos_q[here, :]) & (pos_k[...] < length[m])
            scores = jnp.where(visible, scores * scale, -1e30)
            raised = jnp.exp(scores - jnp.max(scores, axis=-1, keepdims=True))
            prob = (raised / jnp.sum(raised, axis=-1, keepdims=True)).astype(BF16)
            probs[m, here, :] = prob
            value = mm(prob, val[m]).astype(BF16).reshape(quarter, tok, DV)
            for i in range(quarter):
                out[order[g * quarter + i], pl.ds(m * tok, tok), :] = value[i]


def attend(order, length, pieces, query_w, latent_w, expand_w, gain, latent_gain, turn, pos):
    blocks = sum(piece.shape[0] for piece in pieces)
    tok, width = pieces[0].shape[1] // MICRO, query_w.shape[0]
    seq = blocks * tok
    small = sds((MICRO, seq, 128))
    return call(
        attend_kernel,
        (sds((blocks, MICRO * tok, DV)), small, small, small, small, small,
         sds((MICRO, seq, R)), sds((MICRO, seq, seq)), sds((MICRO, seq, 1), F32),
         sds((MICRO, tok, R), F32)),
        [pltpu.SMEM] * 2 + [pl.ANY] * TREE + [pltpu.VMEM] * 8,
        [pltpu.VMEM((blocks, tok, width), BF16), pltpu.SemaphoreType.DMA((TREE,))],
        2 * MICRO * seq * (width * 896 + R * 256 + seq * 384),
        2 * MICRO * seq * (width + seq + 1200) + 1800 * width,
        order, length, *pieces, query_w, latent_w, expand_w, gain.reshape(1, -1),
        latent_gain.reshape(1, -1), turn, pos.reshape(seq, 1), pos.reshape(1, seq),
    )


def attend_back_kernel(order, *refs):
    pieces = refs[:TREE]
    (grad, q_nope, q_rot, k_nope, k_rot, val, latent_n, probs, factor, query_w, expand_w, gain,
     turn) = refs[TREE : TREE + 13]
    (grad_queries, l0, l1, l2, l3, l4, grad_query_w, grad_expand_w, part,
     x, prob_all, grad_k, grad_r, grad_v, sems, prob_sem) = refs[TREE + 13 :]
    blocks, tok, width = x.shape
    quarter = blocks // 4
    span = quarter * tok
    scale = (DN + DR) ** (-0.5)
    grad_query_w[...] = jnp.zeros_like(grad_query_w)
    part[...] = jnp.zeros_like(part)
    lane = lax.broadcasted_iota(jnp.int32, (1, 128), 1)
    for m in range(MICRO):
        load = pltpu.make_async_copy(probs.at[m], prob_all, prob_sem)
        run(tree_copies(pieces, x, sems, m) + [load])
        grad_k[...] = jnp.zeros_like(grad_k)
        grad_r[...] = jnp.zeros_like(grad_r)
        grad_v[...] = jnp.zeros_like(grad_v)

        @pl.loop(0, 4)
        def _(g):
            here = pl.ds(pl.multiple_of(g * span, span), span)
            above = jnp.concatenate(
                [grad[order[g * quarter + i], pl.ds(m * tok, tok), :] for i in range(quarter)],
                axis=0,
            )
            prob_low = prob_all[here, :]
            prob = prob_low.astype(F32)
            weighted = prob * mm_t(above, val[m])
            slope = (weighted - prob * jnp.sum(weighted, axis=-1, keepdims=True)).astype(BF16)
            grad_k[...] += t_mm(slope, q_nope[m, here, :])
            grad_r[...] += t_mm(slope, q_rot[m, here, :])
            grad_v[...] += t_mm(prob_low, above)
            nope = (mm(slope, k_nope[m]) * scale).astype(BF16)
            turned = mm(slope, k_rot[m]) * (scale * turn[here, :])
            grad_q = jnp.concatenate([nope, turned.astype(BF16)], axis=1)
            back = jnp.where(
                lane < DR // 2,
                turned + pltpu.roll(turned, DR // 2, 1),
                turned - pltpu.roll(turned, 128 - DR // 2, 1),
            )
            both = jnp.concatenate([nope, back.astype(BF16)], axis=1).reshape(quarter, tok, 256)
            for i in range(quarter):
                grad_queries[order[g * quarter + i], pl.ds(m * tok, tok), :] = both[i]
            value = rows_of(x, g * quarter, quarter).astype(F32) * factor[m, here, :]
            grad_query_w[...] += t_mm((value * gain[...]).astype(BF16), grad_q)
            normed = mm_t(grad_q, query_w[...])
            part[...] += jnp.sum(normed * value, axis=0, keepdims=True)

        grad_kv = jnp.concatenate([grad_k[...] * scale, grad_v[...]], axis=1).astype(BF16)
        expand_sum = t_mm(latent_n[m], grad_kv)
        grad_expand_w[...] = expand_sum if m == 0 else grad_expand_w[...] + expand_sum
        latent = jnp.concatenate(
            [mm_t(grad_kv, expand_w[...]).astype(BF16), (grad_r[...] * scale).astype(BF16)], axis=1
        ).reshape(blocks, tok, R + 128)
        at = 0
        for ref in (l0, l1, l2, l3, l4):
            count = ref.shape[0]
            ref[:, pl.ds(m * tok, tok), :] = latent[at : at + count]
            at += count


def attend_back(order, pieces, grad, saved, query_w, expand_w, gain, turn, marks):
    blocks = sum(piece.shape[0] for piece in pieces)
    both, width = pieces[0].shape[1], query_w.shape[0]
    tok = both // MICRO
    seq = blocks * tok
    quarter = blocks // 4
    sizes = (quarter,) * 3 + (quarter // 2,) * 2
    return call(
        attend_back_kernel,
        (sds((blocks, both, 256)),)
        + tuple(sds((count, both, R + 128)) for count in sizes)
        + (sds((width, 256), F32), sds((R, 256), F32), sds((1, width), F32)),
        [pltpu.SMEM] + [pl.ANY] * TREE + [pltpu.VMEM] * 7 + [pl.ANY] + [pltpu.VMEM] * 5,
        [pltpu.VMEM((blocks, tok, width), BF16), pltpu.VMEM((seq, seq), BF16)]
        + [pltpu.VMEM((seq, 128), F32)] * 3
        + [pltpu.SemaphoreType.DMA((TREE,)), pltpu.SemaphoreType.DMA],
        2 * MICRO * seq * (width * 512 + R * 512 + seq * 768),
        2 * MICRO * seq * (2 * width + seq + 2000) + 2 * query_w.size,
        order, *pieces, grad, *saved[1:9], query_w, expand_w, gain.reshape(1, -1), turn,
        marks=marks,
    )


def early_kernel(m, *refs):
    pieces = refs[:TREE]
    pick, row_gate, down, shared_down, back, grad_eh, grad_shared, whole, g, sems = refs[TREE:]
    blocks, tok, width = g.shape
    quarter = blocks // 4
    room = pick.shape[1]
    run(tree_copies(pieces, g, sems, m))

    @pl.loop(0, 4)
    def _(q):
        value = rows_of(g, q * quarter, quarter)
        here = pl.ds(pl.multiple_of(q * room, room), room)
        back[here, :] = (row_gate[here, :] * mm(pick[q], value)).astype(BF16)
        span = quarter * tok
        there = pl.ds(pl.multiple_of(q * span, span), span)
        grad_shared[there, :] = mm_t(value, shared_down[...])
        whole[there, :] = value

    chunks = down.shape[0] // 128

    @pl.loop(0, chunks)
    def _(f):
        here = pl.ds(pl.multiple_of(f * 128, 128), 128)
        grad_eh[:, here] = mm_t(back[...], down[here, :])


def early(m, pieces, pick, row_gate, down, shared_down, marks):
    blocks = sum(piece.shape[0] for piece in pieces)
    tok, width = pieces[0].shape[1] // MICRO, down.shape[1]
    rows, units = pick.shape[0] * pick.shape[1], shared_down.shape[0]
    return call(
        functools.partial(early_kernel, m),
        (sds((rows, width)), sds((rows, down.shape[0]), F32), sds((blocks * tok, units), F32),
         sds((blocks * tok, width))),
        [pl.ANY] * TREE + [pltpu.VMEM] * 4,
        [pltpu.VMEM((blocks, tok, width), BF16), pltpu.SemaphoreType.DMA((TREE,))],
        2 * rows * width * (down.shape[0] + 256),
        2 * width * (2 * blocks * tok + rows + down.shape[0]) + 4 * rows * down.shape[0],
        *pieces, pick, row_gate, down, shared_down, marks=marks,
    )


def expert_kernel(m, *refs):
    pieces = refs[:TREE]
    pick, grad_eh, grad_shared, both, share_g, share_u = refs[TREE : TREE + 6]
    first = TREE + 6 + (TREE if m else 0)
    mixed, arrived, hidden, grad_gu, shared_hidden, grad_sg, grad_su = refs[first : first + 7]
    outs = refs[first + 7 : first + 7 + TREE]
    x, w, o, sems, w_sems = refs[first + 7 + TREE :]
    blocks, tok, width = x.shape
    quarter = blocks // 4
    span = quarter * tok
    room = pick.shape[1]
    chunks = w.shape[0] // 256
    copies = tree_copies(pieces, x, sems, m)
    for copy in copies:
        copy.start()
    loads = [
        pltpu.make_async_copy(both.at[pl.ds(f * 256, 256)], w.at[pl.ds(f * 256, 256)], w_sems.at[f])
        for f in range(chunks)
    ]
    for copy in loads:
        copy.start()
    for copy in copies:
        copy.wait()

    @pl.loop(0, 4)
    def _(q):
        value = rows_of(x, q * quarter, quarter)
        there = pl.ds(pl.multiple_of(q * span, span), span)
        here = pl.ds(pl.multiple_of(q * room, room), room)
        mixed[there, :] = value
        arrived[here, :] = mm(pick[q], value).astype(BF16)
        gate = mm(value, share_g[...])
        lift = mm(value, share_u[...])
        sigma = 1.0 / (1.0 + jnp.exp(-gate))
        grad = grad_shared[there, :]
        shared_hidden[there, :] = (gate * sigma * lift).astype(BF16)
        grad_sg[there, :] = (grad * lift * sigma * (1.0 + gate * (1.0 - sigma))).astype(BF16)
        grad_su[there, :] = (grad * gate * sigma).astype(BF16)

    for copy in loads:
        copy.wait()

    @pl.loop(0, chunks)
    def _(f):
        rows = pl.ds(pl.multiple_of(f * 256, 256), 256)
        cols = pl.ds(pl.multiple_of(f * 128, 128), 128)
        value = mm_t(arrived[...], w[rows, :])
        gate, lift = value[:, :128], value[:, 128:]
        sigma = 1.0 / (1.0 + jnp.exp(-gate))
        grad = grad_eh[:, cols]
        hidden[:, cols] = (gate * sigma * lift).astype(BF16)
        grad_gu[:, rows] = jnp.concatenate(
            [
                (grad * lift * sigma * (1.0 + gate * (1.0 - sigma))).astype(BF16),
                (grad * gate * sigma).astype(BF16),
            ],
            axis=1,
        )

    spread_out(
        o, pick, 512,
        lambda cols: mm(grad_gu[...], w[:, cols]).astype(BF16),
        lambda there, cols: mm_t(grad_sg[there, :], share_g[cols, :])
        + mm_t(grad_su[there, :], share_u[cols, :]),
    )
    run(tree_copies(outs, o, sems, m, True))


def spread_out(o, pick, step, routed, shared):
    blocks, tok, width = o.shape
    quarter = blocks // 4
    span = quarter * tok
    room = pick.shape[1]

    @pl.loop(0, width // step)
    def _(c):
        cols = pl.ds(pl.multiple_of(c * step, step), step)
        value = routed(cols)
        for q in range(4):
            there = pl.ds(q * span, span)
            tokens = t_mm(pick[q], value[q * room : (q + 1) * room]) + shared(there, cols)
            o[pl.ds(q * quarter, quarter), :, cols] = tokens.astype(BF16).reshape(
                quarter, tok, step
            )


def experts(m, pieces, pick, grad_eh, grad_shared, both, share_g, share_u, earlier):
    blocks = sum(piece.shape[0] for piece in pieces)
    tok, width = pieces[0].shape[1] // MICRO, pieces[0].shape[2]
    seq, rows, units = blocks * tok, pick.shape[0] * pick.shape[1], share_g.shape[1]
    hid = both.shape[0] // 2
    whole = pltpu.VMEM((blocks, tok, width), BF16)
    return call(
        functools.partial(expert_kernel, m),
        (sds((seq, width)), sds((rows, width)), sds((rows, hid)), sds((rows, 2 * hid)))
        + (sds((seq, units)),) * 3 + tuple(sds(piece.shape) for piece in pieces),
        [pl.ANY] * TREE + [pltpu.VMEM] * 3 + [pl.ANY] + [pltpu.VMEM] * 2
        + [pl.ANY] * len(earlier),
        [whole, pltpu.VMEM(both.shape, BF16), whole,
         pltpu.SemaphoreType.DMA((TREE,)), pltpu.SemaphoreType.DMA((both.shape[0] // 256,))],
        8 * rows * width * hid + 8 * seq * width * 256,
        2 * both.size + 6 * seq * width + 10 * rows * hid,
        *pieces, pick, grad_eh, grad_shared, both, share_g, share_u, *earlier,
        outs=[pltpu.VMEM] * 7 + [pl.ANY] * TREE,
        aliases={TREE + 6 + i: 7 + i for i in range(len(earlier))},
    )


def output_kernel(m, *refs):
    hidden, row_gate, pick, down, shared_hidden, shared_down = refs[:6]
    first = 6 + (TREE if m else 0)
    outs = refs[first : first + TREE]
    o, sems = refs[first + TREE :]
    spread_out(
        o, pick, 512,
        lambda cols: (
            row_gate[...] * mm(hidden[...], down[:, cols]).astype(BF16).astype(F32)
        ).astype(BF16),
        lambda there, cols: mm(shared_hidden[there, :], shared_down[:, cols]),
    )
    run(tree_copies(outs, o, sems, m, True))


def expert_output(m, pieces, hidden, row_gate, pick, down, shared_hidden, shared_down, earlier,
                  marks):
    blocks = sum(piece.shape[0] for piece in pieces)
    tok, width = pieces[0].shape[1] // MICRO, pieces[0].shape[2]
    return call(
        functools.partial(output_kernel, m),
        tuple(sds(piece.shape) for piece in pieces),
        [pltpu.VMEM] * 6 + [pl.ANY] * len(earlier),
        [pltpu.VMEM((blocks, tok, width), BF16), pltpu.SemaphoreType.DMA((TREE,))],
        2 * hidden.size * width + 4 * blocks * tok * 256 * width,
        2 * down.size + 2 * hidden.size + 2 * blocks * tok * width,
        hidden, row_gate, pick, down, shared_hidden, shared_down, *earlier,
        marks=marks,
        outs=[pl.ANY] * TREE,
        aliases={6 + i: i for i in range(len(earlier))},
    )


def weight_kernel(reps, count, *refs):
    l0, l1, r0, r1, *outs = refs[count:]
    unit = 128 // reps
    value = t_mm(l0[...], r0[...]) + t_mm(l1[...], r1[...])
    for index, ref in enumerate(outs):
        for part in range(reps):
            start = index * 128 + part * unit
            ref[part] = value[start : start + unit].astype(ref.dtype)


def weight_sums(reps, lanes, left, right, marks):
    rows, width = right[0].shape
    hid = left[0].shape[1] * 128 // lanes
    chunks, unit = hid // 128, 128 // reps
    whole = pl.BlockSpec((rows, width), lambda f: (0, 0), pipeline_mode=pl.Buffered(1))
    part = pl.BlockSpec((reps, unit, width), lambda f: (0, f, 0))
    return pl.pallas_call(
        functools.partial(weight_kernel, reps, len(marks)),
        grid=(chunks,),
        in_specs=[pl.BlockSpec(memory_space=pl.ANY)] * len(marks)
        + [pl.BlockSpec((rows, lanes), lambda f: (0, f))] * 2 + [whole] * 2,
        out_specs=[part] * (lanes // 128),
        out_shape=[sds((reps, hid // reps, width))] * (lanes // 128),
        compiler_params=pltpu.CompilerParams(vmem_limit_bytes=LIMIT),
        cost_estimate=pl.CostEstimate(
            flops=4 * rows * width * hid * lanes // 128,
            bytes_accessed=10 * width * hid,
            transcendentals=0,
        ),
    )(*marks, *left, *right)


def rep_pull(value, count, step):
    return lax.ppermute(value, "rep", [((d + step) % count, d) for d in range(count)])


def rep_parts(value, count):
    return [value] + [rep_pull(value, count, step) for step in range(1, count)]


def rep_total(parts, count):
    value = parts[0].astype(F32)
    for step in range(1, count):
        perm = [(d, (d + step) % count) for d in range(count)]
        value = value + lax.ppermute(parts[step], "rep", perm).astype(F32)
    return value


def rep_sum(value):
    return jnp.sum(lax.all_gather(value.astype(BF16), "rep", axis=0).astype(F32), axis=0)


def body(
    hidden_in,
    cotangent,
    lengths,
    routes,
    gate_values,
    attn_gain,
    query_proj,
    latent_proj,
    latent_gain,
    expand_proj,
    output_proj,
    ffn_gain,
    shared_gate,
    shared_lift,
    shared_down,
    expert_gate,
    expert_lift,
    expert_down,
):
    tok = hidden_in.shape[1]
    width = hidden_in.shape[2]
    n = lax.axis_size("fsdp")
    reps = lax.axis_size("rep")
    me = lax.axis_index("fsdp")
    rep = lax.axis_index("rep")
    outer = n // 4
    seq = tok * n
    capacity = min(tok, 3 * tok * TOP // (2 * n))
    split = max(1, n // H)
    rows = width // n

    slots = jnp.arange(n, dtype=jnp.int32)
    nearness = near_first(outer)
    steps_on = jnp.asarray(nearness, jnp.int32)
    place_of = jnp.asarray([nearness.index(k) for k in range(outer)], jnp.int32)
    abs_of_rel = ((me // 4 + steps_on[slots % outer]) % outer) * 4 + ((me % 4) ^ (slots // outer))
    rel_of_abs = ((slots % 4) ^ (me % 4)) * outer + place_of[(slots // 4 - me // 4) % outer]
    rep_order = (jnp.arange(reps, dtype=jnp.int32) - rep) % reps
    own_pos = me * tok + jnp.arange(tok, dtype=jnp.int32)
    pos = (abs_of_rel[:, None] * tok + jnp.arange(tok, dtype=jnp.int32)[None, :]).reshape(seq)
    freqs = THETA ** (-(2.0 * jnp.arange(DR // 2, dtype=F32)) / DR)
    angles = pos.astype(F32)[:, None] * freqs[None, :]
    cosine, sine = jnp.cos(angles), jnp.sin(angles)
    turn = jnp.concatenate([cosine, cosine, sine, sine], axis=1)

    def all_to_all(value):
        return lax.all_to_all(value, "fsdp", split_axis=0, concat_axis=0, tiled=True)

    def rep_slice(value, axis):
        size = value.shape[axis] // reps
        return lax.dynamic_slice_in_dim(value, rep * size, size, axis)

    def rep_join(value, axis):
        parts = jnp.take(jnp.stack(rep_parts(value, reps)), rep_order, axis=0)
        return jnp.concatenate([parts[i] for i in range(reps)], axis=axis)

    def unreshard(value):
        return rep_sum(all_to_all(value.astype(BF16)))

    def by_head(value):
        return jnp.repeat(value, split, axis=0) if split > 1 else value

    both = MICRO * tok
    dense_gate = jnp.sum(
        jnp.where(routes[..., None] == slots, gate_values[..., None], 0.0), axis=2
    ).reshape(both, n)
    gate_high = dense_gate.astype(BF16)
    gate_low = (dense_gate - gate_high.astype(F32)).astype(BF16)

    def fit(value):
        return jnp.pad(value, ((0, both - value.shape[0]), (0, 0)))

    items = [
        fit(latent_proj),
        gate_high,
        gate_low,
        fit(attn_gain[:, None]),
        fit(ffn_gain[:, None]),
        fit(latent_gain[:, None]),
    ]
    starts = [0]
    for item in items:
        starts.append(starts[-1] + item.shape[1])
    fill = jnp.zeros((both, -starts[-1] % 128), BF16)
    small = gather_small("small", jnp.concatenate(items + [fill], axis=1), n)[0]
    extras = jnp.concatenate(small, axis=0)
    latent_w = jnp.take(extras[:, :rows, : starts[1]], rel_of_abs, axis=0).reshape(width, R + DR)
    gates = extras[..., starts[1] : starts[3]].reshape(n, both, 2, n).astype(F32)
    gates = jnp.sum(jnp.where(slots == me, gates, 0.0), axis=(2, 3))
    gains = jnp.take(extras[..., starts[3] : starts[6]], rel_of_abs, axis=0).astype(F32)
    gains = jnp.transpose(gains, (2, 0, 1))
    attn_gain_f = gains[0, :, :rows].reshape(width)
    ffn_gain_f = gains[1, :, :rows].reshape(width)
    latent_gain_f = gains[2, :, : R // n].reshape(R)

    head_w = jnp.concatenate(
        [
            jnp.transpose(query_proj.reshape(rows, H, DN + DR), (1, 0, 2)),
            jnp.transpose(expand_proj.reshape(R // n, H, DN + DV), (1, 0, 2)).reshape(
                H, rows, -1
            ),
        ],
        axis=2,
    )
    head_w = all_to_all(by_head(head_w))
    query_w = head_w[..., : DN + DR].reshape(width, DN + DR)
    expand_w = head_w[..., DN + DR :].reshape(R, DN + DV)
    query_w = jnp.concatenate([query_w] + swapped(query_w[:, DN:]), axis=1)
    latent_in = jnp.concatenate([latent_w] + swapped(latent_w[:, R:]), axis=1)

    unit = 128 // reps

    def chunked(*weights):
        parts = [lax.all_gather(item, "rep", axis=0) for item in weights]
        return jnp.stack(
            [part[i].reshape(-1, unit, width) for part in parts for i in range(reps)], axis=1
        ).reshape(-1, width)

    both_w = chunked(jnp.swapaxes(expert_gate[0], 0, 1), jnp.swapaxes(expert_lift[0], 0, 1))
    down_w = chunked(expert_down[0])
    block = hidden_in.reshape(both, width)
    hidden_all, given = gather_tree(
        "hidden", block, n, ((), (), [query_w, latent_in, expand_w, both_w, down_w])
    )
    query_w, latent_in, expand_w, both_w, down_w = given[2]

    cols = width // reps
    used = (own_pos[None, :] < lengths[:, None])[..., None]
    grad_rows = jnp.where(used, cotangent, jnp.zeros_like(cotangent)).reshape(both, width)
    (out_share,), hidden_all[1:2] = order_after([rep_slice(output_proj, 1)], hidden_all[1:2])
    out_marks = hidden_all[3:4]
    att = attend(
        abs_of_rel, lengths, hidden_all, query_w, latent_in, expand_w,
        attn_gain_f, latent_gain_f, turn, pos,
    )
    att = list(att)

    out_pieces, _, att[0:1] = gather_small("output_w", out_share, n, out_marks, att[0:1])
    heads_out = all_to_all(att[0])
    (grad_rows,), out_pieces[0:1] = order_after([grad_rows], out_pieces[0:1])
    grad_all, given = gather_tree("cotangent", grad_rows, n, (out_pieces[1:3] + [heads_out], (), ()))
    out_pieces[1], out_pieces[2], heads_out = given[0]
    heads_out = heads_out[::split]
    heads_local = jnp.transpose(heads_out, (1, 0, 2)).reshape(both, n, H * DV // n)
    heads_local = jnp.take(heads_local, abs_of_rel, axis=1).reshape(both, H * DV)
    cols = width // reps
    out_w = rep_parts(jnp.concatenate(out_pieces, axis=0).reshape(H * DV, cols), reps)

    def columns(step):
        return ((rep + step) % reps) * cols

    merge = 1
    while (merge * capacity) % 16:
        merge *= 2
    groups = n // merge
    span = merge * tok
    room = merge * capacity
    upper = (jnp.arange(span)[:, None] <= jnp.arange(span)[None, :]).astype(BF16)

    hidden = hidden_in.reshape(both, width).astype(F32)
    residual = jnp.zeros((both, width), F32)
    for step in range(reps):
        share = contract("tj,jd->td", heads_local, out_w[step])
        residual = lax.dynamic_update_slice(residual, share, (0, columns(step)))
    residual = hidden + residual
    mixed, inv_second = rms_forward(residual, ffn_gain_f)
    mixed = mixed.astype(BF16)
    (shared_gate, shared_lift), (mixed,) = order_after([shared_gate, shared_lift], [mixed])

    ahead = []
    for m in range(MICRO):
        gate_here = gates[:, m * tok : (m + 1) * tok].reshape(groups, span)
        hit = gate_here > 0.0
        place = contract("gt,ts->gs", hit.astype(BF16), upper).astype(jnp.int32) - 1
        chosen = hit[:, None, :] & (
            place[:, None, :] == jnp.arange(room, dtype=jnp.int32)[None, :, None]
        )
        pick = chosen.astype(BF16)
        row_gate = jnp.sum(jnp.where(chosen, gate_here[:, None, :], 0.0), axis=2).reshape(-1, 1)
        ahead.append(
            (pick, row_gate) + early(m, grad_all, pick, row_gate, down_w, shared_down,
                    (ahead[0][2],) if m else (mixed,))
        )

    shared_in = jnp.concatenate(
        [
            jnp.transpose(shared_gate.reshape(rows, n, -1), (1, 0, 2)),
            jnp.transpose(shared_lift.reshape(rows, n, -1), (1, 0, 2)),
        ],
        axis=2,
    )
    units = shared_in.shape[2] // 2
    shared_in = all_to_all(shared_in)
    marks = [list(item) for item in ahead]
    mixed_all, given = gather_tree(
        "mixed", mixed, n, ((), [marks[0][2], shared_in, both_w], [marks[1][2]])
    )
    marks[0][2], shared_in, both_w = given[1]
    marks[1][2:3] = given[2]
    shared_in = shared_in.reshape(width, 2 * units)
    ahead = marks

    share_g, share_u = shared_in[:, :units], shared_in[:, units:]

    share = jnp.concatenate([rep_slice(query_proj, 1)], axis=1)
    (share,), mixed_all[8:] = order_after([share], mixed_all[8:])
    whole_query = lax.all_gather(share, "fsdp", axis=0, tiled=True)

    done = []
    earlier = ()
    for m in range(MICRO):
        pick, row_gate, back, grad_eh, grad_shared, _ = ahead[m]
        done.append(
            experts(m, mixed_all, pick, grad_eh, grad_shared, both_w, share_g, share_u, earlier)
        )
        earlier = done[m][7:]
    earlier = list(earlier)
    pieces = ()
    halves = scatter_tree_last("grad_mixed", earlier, n)
    bases = scatter_tree_cross("grad_mixed", halves, n)
    stages = [(halves[0][1],), (halves[1][2],), (bases[0][0],), (bases[1][0],)]
    for m in range(MICRO):
        pick, row_gate = ahead[m][:2]
        pieces = list(
            expert_output(
                m, mixed_all, done[m][2], row_gate, pick, down_w, done[m][4], shared_down,
                pieces, stages[2 * m],
            )
        )
        if m == 0:
            down_sums = list(
                weight_sums(
                    reps, 128, (done[0][2], done[1][2]), (ahead[0][2], ahead[1][2]),
                    stages[1] + (pieces[0],),
                )
            )
            share_grads, down_sums[0:1] = order_after(
                [done[0][5], done[1][5]], list(down_sums[0:1])
            )
            stages[2] += (down_sums[0],)
    down_sums = list(down_sums)
    both_sums = weight_sums(
        reps, 256, (done[0][3], done[1][3]), (done[0][1], done[1][1]),
        stages[3] + (pieces[0],),
    )
    both_sums = list(both_sums)
    grad_mixed, _ = scatter_tree_rest("grad_mixed", bases, n)
    grad_shared_in = sum(
        contract("td,tf->df", done[m][0], jnp.concatenate([share_grads[m], done[m][6]], axis=1))
        for m in range(MICRO)
    )
    grad_shared_in = all_to_all(grad_shared_in.astype(BF16).reshape(n, rows, 2 * units))
    (grad_mixed,), (both_sums[0], grad_shared_in) = order_after(
        [grad_mixed], [both_sums[0], grad_shared_in]
    )
    whole_query = lax.all_gather(whole_query, "rep", axis=0)
    expert_sums = [
        lax.psum_scatter(item, "rep", scatter_dimension=0) for item in both_sums + down_sums
    ]
    grad_res, part_ffn = rms_backward(residual, inv_second, ffn_gain_f, grad_mixed)
    grad_res = grad_res + grad_rows.astype(F32)
    grad_res_low = grad_res.astype(BF16)
    grad_heads = sum(
        contract(
            "td,jd->tj",
            lax.dynamic_slice_in_dim(grad_res_low, columns(step), cols, 1),
            out_w[step],
        )
        for step in range(reps)
    )
    grad_heads = jnp.take(
        grad_heads.astype(BF16).reshape(both, n, H * DV // n), rel_of_abs, axis=1
    )
    grad_heads = jnp.transpose(grad_heads.reshape(both, H, DV), (1, 0, 2))
    grad_heads = by_head(grad_heads)
    grad_heads = all_to_all(grad_heads)
    if split > 1:
        grad_heads = jnp.where(me % split == 0, grad_heads, jnp.zeros_like(grad_heads))

    shares = []
    for step in range(reps):
        piece = lax.dynamic_slice_in_dim(grad_res_low, columns(step), cols, 1)
        shares.append(contract("tj,td->jd", heads_local, piece))
    out_total = rep_total([shares[0]] + [item.astype(BF16) for item in shares[1:]], reps)
    out_total = out_total.astype(BF16).reshape(n, rows, cols)
    out_pieces = small_split(out_total)

    result = attend_back(
        abs_of_rel, hidden_all, grad_heads, att, query_w, expand_w, attn_gain_f, turn,
        [whole_query] + expert_sums,
    )
    result = list(result)
    pieces[6:], result[6:7] = order_after(pieces[6:], result[6:7])
    halves = scatter_tree_last("routed", pieces, n)
    expert_sums, result[1:2] = order_after(expert_sums, result[1:2])
    grad_expert_gate, grad_expert_lift, grad_expert_down = [
        item.astype(F32) for item in expert_sums
    ]
    (grad_shared_in,), result[2:3] = order_after([grad_shared_in], result[2:3])
    grad_shared_in = rep_sum(grad_shared_in)
    grad_shared_gate = jnp.transpose(grad_shared_in[:, :, :units], (1, 0, 2)).reshape(rows, -1)
    grad_shared_lift = jnp.transpose(grad_shared_in[:, :, units:], (1, 0, 2)).reshape(rows, -1)
    down_sum = sum(contract("tf,td->fd", done[m][4], ahead[m][5]) for m in range(MICRO))
    grad_shared_down = rep_sum(down_sum)


    bases = scatter_tree_cross("routed", halves, n)
    grad_queries = all_to_all(result[0])
    grad_latent = scatter_small_last("grad_latent", result[1:6], n)
    grad_latent, (grad_queries,) = scatter_small_rest(
        "grad_latent", grad_latent, n, [grad_queries]
    )
    routed, (grad_latent,) = scatter_tree_rest("routed", bases, n, [grad_latent])
    outputs = (residual + routed).astype(BF16).reshape(MICRO, tok, width)
    out_pieces[3:], (grad_latent,) = order_after(out_pieces[3:], [grad_latent])
    out_pieces = scatter_small_last("grad_output_w", out_pieces, n)
    grad_q, grad_expand_w, part_attn = result[6:]

    latent = att[9].reshape(both, R)
    inv = lax.rsqrt(jnp.mean(latent * latent, axis=-1, keepdims=True) + EPS)
    grad_c, part_latent = rms_backward(latent, inv, latent_gain_f, grad_latent[:, :R])
    own_cos, own_sin = jnp.tile(cosine[:tok], (MICRO, 1)), jnp.tile(sine[:tok], (MICRO, 1))
    grad_krope = rotate_back(grad_latent[:, R : R + DR], own_cos, own_sin)
    grad_kva = jnp.concatenate([grad_c, grad_krope], axis=1).astype(BF16)
    grad_local = contract("tj,dj->td", grad_kva, latent_w)
    factor = att[8][:, :tok].reshape(both, 1)
    part_attn = part_attn[0] + jnp.sum(grad_local * hidden * factor, axis=0)

    gain_parts = jnp.stack(
        [
            part_attn.reshape(n, rows),
            part_ffn.reshape(n, rows),
            jnp.pad(part_latent.reshape(n, R // n), ((0, 0), (0, rows - R // n))),
        ],
        axis=1,
    )
    kv_pieces = gather_small("grad_kv", grad_kva, n)[0]

    turn_part = grad_q[:, DN + DR :]
    half = DR // 2
    grad_q = jnp.concatenate(
        [
            grad_q[:, :DN],
            grad_q[:, DN : DN + half] + turn_part[:, half:],
            grad_q[:, DN + half : DN + DR] - turn_part[:, :half],
        ],
        axis=1,
    )
    head_grad = jnp.concatenate(
        [grad_q.reshape(n, rows, DN + DR), grad_expand_w.reshape(n, rows, -1)], axis=2
    ).astype(BF16)
    gain_high = gain_parts.astype(BF16)
    gain_low = (gain_parts - gain_high.astype(F32)).astype(BF16)
    gain_rows = jnp.stack([gain_high, gain_low], axis=1).reshape(n, -1)
    gain_count = gain_rows.shape[1]
    head_cols = head_grad.shape[2]
    gain_rows = jnp.pad(gain_rows, ((0, 0), (0, 16 * head_cols - gain_count)))
    head_grad = jnp.concatenate([head_grad, gain_rows.reshape(n, 16, head_cols)], axis=1)
    (head_grad,), (grad_queries,) = order_after([head_grad], [grad_queries])
    head_grad = all_to_all(head_grad)
    gain_sum = head_grad[:, rows:].reshape(n, -1)[:, :gain_count].astype(F32)
    gain_sum = jnp.sum(gain_sum, axis=0).reshape(2, 3, rows)
    gain_sum = gain_sum[0] + gain_sum[1]
    head_grad = head_grad[:, :rows]
    out_sum, _ = scatter_small_rest("grad_output_w", out_pieces, n)
    (head_grad,), kv_pieces[1:2] = order_after([head_grad], kv_pieces[1:2])
    head_grad = rep_sum(head_grad)[::split]
    grad_output_proj = rep_join(out_sum.astype(BF16), 1).astype(F32)
    grad_queries = jnp.transpose(grad_queries[::split, :, : DN + DR], (1, 0, 2))
    grad_queries = grad_queries.reshape(both, reps, -1)
    grad_normed = sum(
        contract("tj,dj->td", grad_queries[:, i], whole_query[i]) for i in range(reps)
    )
    grad_first, _ = rms_backward(hidden, factor, attn_gain_f, grad_normed + grad_local)
    input_grads = (grad_first + grad_res).astype(BF16).reshape(MICRO, tok, width)

    grad_query_proj = jnp.transpose(head_grad[..., : DN + DR], (1, 0, 2)).reshape(rows, -1)
    grad_expand_proj = jnp.transpose(
        head_grad[..., DN + DR :].reshape(H, R // n, DN + DV), (1, 0, 2)
    ).reshape(R // n, H * (DN + DV))

    kv_blocks = jnp.concatenate(kv_pieces, axis=0)
    hidden_all, (grad_queries,) = order_after(hidden_all, [grad_queries])
    gain_cols = lax.dynamic_slice_in_dim(attn_gain_f, me * rows, rows, 0)
    hidden_cols = jnp.concatenate(
        [lax.dynamic_slice_in_dim(item, me * rows, rows, 2) for item in hidden_all], axis=0
    ).reshape(n, MICRO, tok, rows)
    factors = jnp.swapaxes(att[8].reshape(MICRO, n, tok, 1), 0, 1)
    normed_cols = (hidden_cols.astype(F32) * factors * gain_cols).astype(BF16)
    latent_total = contract(
        "tj,td->jd", kv_blocks.reshape(-1, R + DR), normed_cols.reshape(-1, rows)
    )
    latent_total = rep_sum(latent_total)
    grad_latent_proj = latent_total.T

    gain_sum = gain_sum + sum(rep_pull(gain_sum, reps, step) for step in range(1, reps))

    return (
        outputs,
        input_grads,
        gain_sum[0],
        grad_query_proj,
        grad_latent_proj,
        gain_sum[2, : R // n],
        grad_expand_proj,
        grad_output_proj,
        gain_sum[1],
        grad_shared_gate,
        grad_shared_lift,
        grad_shared_down,
        jnp.swapaxes(grad_expert_gate, 0, 1)[None],
        jnp.swapaxes(grad_expert_lift, 0, 1)[None],
        grad_expert_down[None],
    )


def solution(mesh):
    in_specs = (
        P("rep", "fsdp", None),
        P("rep", "fsdp", None),
        P("rep"),
        P("rep", "fsdp", None),
        P("rep", "fsdp", None),
        P("fsdp"),
        P("fsdp", None),
        P("fsdp", None),
        P("fsdp"),
        P("fsdp", None),
        P("fsdp", None),
        P("fsdp"),
        P("fsdp", None),
        P("fsdp", None),
        P("fsdp", None),
        P("fsdp", None, "rep"),
        P("fsdp", None, "rep"),
        P("fsdp", "rep", None),
    )
    out_specs = (
        P("rep", "fsdp", None),
        P("rep", "fsdp", None),
        P("fsdp"),
        P("fsdp", None),
        P("fsdp", None),
        P("fsdp"),
        P("fsdp", None),
        P("fsdp", None),
        P("fsdp"),
        P("fsdp", None),
        P("fsdp", None),
        P("fsdp", None),
        P("fsdp", None, "rep"),
        P("fsdp", None, "rep"),
        P("fsdp", "rep", None),
    )
    return jax.shard_map(body, mesh=mesh, in_specs=in_specs, out_specs=out_specs, check_vma=False)
```

```python
import functools

import jax
import jax.numpy as jnp
from jax import lax
from jax.experimental import pallas as pl
from jax.experimental.pallas import tpu as pltpu
from jax.sharding import PartitionSpec as P

H = 16
DN = 128
DR = 64
DV = 128
R = 512
TOP = 6
MICRO = 2

EPS = 1e-06
THETA = 10000.0
F32 = jnp.float32
BF16 = jnp.bfloat16


def contract(form, left, right):
    return jnp.einsum(form, left, right, preferred_element_type=F32)


def rms_forward(value, gain):
    factor = lax.rsqrt(jnp.mean(value * value, axis=-1, keepdims=True) + EPS)
    return (value * factor * gain, factor)


def rms_backward(value, factor, gain, grad):
    scaled = grad * gain
    inner = jnp.mean(value * scaled, axis=-1, keepdims=True)
    return (
        factor * scaled - value * factor * factor * factor * inner,
        jnp.sum(grad * value * factor, axis=0),
    )


def rotate_back(grad, cosine, sine):
    half = grad.shape[-1] // 2
    first = grad[..., :half]
    second = grad[..., half:]
    return jnp.concatenate(
        [first * cosine + second * sine, second * cosine - first * sine], axis=-1
    )


def swapped(weight):
    half = weight.shape[1] // 2
    return [-weight[:, half:], weight[:, :half]]


def named(function):
    def scoped(name, *args):
        with jax.named_scope(name):
            return function(*args)

    return scoped


def near_first(outer):
    return [0] + [k for _, k in sorted((min(k, outer - k), k) for k in range(1, outer))]


def partners(devices, q, k):
    outer = devices // 4
    return [(d, ((d // 4 + k) % outer) * 4 + ((d % 4) ^ q)) for d in range(devices)]


def pull(value, devices, q, k=0):
    perm = [(there, here) for here, there in partners(devices, q, k)]
    return lax.ppermute(value, "fsdp", perm)


def push(value, devices, q, k=0):
    return lax.ppermute(value, "fsdp", partners(devices, q, k))


def order_after(values, marks):
    values, marks = list(values), list(marks)
    if not marks:
        return values, marks
    both = lax.optimization_barrier(tuple(values + marks))
    return list(both[: len(values)]), list(both[len(values) :])


def total(first, *others):
    value = first.astype(F32)
    for item in others:
        value = value + item.astype(F32)
    return value


@named
def gather_small(block, devices, cross_marks=(), last_marks=()):
    outer = devices // 4
    half = outer // 2
    base = jnp.stack([block] + [pull(block, devices, 0, k) for k in near_first(outer)[1:]])
    (sent,), cross_marks = order_after([base], cross_marks)
    one = pull(sent, devices, 1)
    two = pull(sent, devices, 2)
    (low, high), last_marks = order_after([one[:half], two[half:]], last_marks)
    low, high = pull(low, devices, 2), pull(high, devices, 1)
    return [base, one, two, low, high], cross_marks, last_marks


@named
def scatter_small_last(pieces, devices):
    base, one, two, low, high = pieces
    half = devices // 8
    low = push(low, devices, 2)
    high = push(high, devices, 1)
    zero = (0,) * one.ndim
    one = lax.dynamic_update_slice(one, total(one[:half], low).astype(BF16), zero)
    two = lax.dynamic_update_slice(
        two, total(two[half:], high).astype(BF16), (half,) + zero[1:]
    )
    return base, one, two


@named
def scatter_small_rest(pieces, devices, marks=()):
    base, one, two = pieces
    outer = devices // 4
    base = total(base, push(one, devices, 1), push(two, devices, 2))
    (sent,), marks = order_after([base[1:].astype(BF16)], marks)
    order = near_first(outer)
    return total(
        base[0], *[push(sent[i - 1], devices, 0, order[i]) for i in range(1, outer)]
    ), marks


@named
def gather_tree(block, devices, marks):
    outer = devices // 4
    half, part = outer // 2, outer // 4
    marks = [list(items) for items in marks]
    held = [block]
    for k in near_first(outer)[1:]:
        held.append(pull(block, devices, 0, k))
    pieces = [[], [], [], []]
    before = []
    for place, base in enumerate((held[:half], held[half:])):
        base = jnp.stack(base)
        if place == 0:
            (base,), marks[0] = order_after([base], marks[0])
        else:
            (base,), given = order_after([base], before + marks[1])
            pieces[1], pieces[2], marks[1] = given[0:1], given[1:2], given[2:]
        one = pull(base, devices, 1)
        two = pull(base, devices, 2)
        before = [one, two]
        low, high = one[:part], two[part:]
        if place:
            (low, high), given = order_after([low, high], pieces[3] + marks[2])
            pieces[3], marks[2] = given[:2], given[2:]
        last = [pull(low, devices, 2), pull(high, devices, 1)]
        for q, items in enumerate(([base], [one], [two], last)):
            pieces[q] += items
    return sum(pieces, []), marks


@named
def scatter_tree_last(pieces, devices):
    part = devices // 16
    halves = []
    for here in (1, 0):
        base, one, two = pieces[here], pieces[2 + here], pieces[4 + here]
        low, high = pieces[6 + 2 * here : 8 + 2 * here]
        low = push(low, devices, 2)
        high = push(high, devices, 1)
        zero = (0,) * one.ndim
        one = lax.dynamic_update_slice(one, total(one[:part], low).astype(BF16), zero)
        two = lax.dynamic_update_slice(
            two, total(two[part:], high).astype(BF16), (part,) + zero[1:]
        )
        halves.append((base, one, two))
    return halves


@named
def scatter_tree_cross(halves, devices):
    bases = []
    for base, one, two in halves:
        one = push(one, devices, 1)
        two = push(two, devices, 2)
        bases.append([total(base[i], one[i], two[i]) for i in range(base.shape[0])])
    return bases


@named
def scatter_tree_rest(bases, devices, marks=()):
    outer = devices // 4
    order = near_first(outer)
    sent, marks = order_after(
        [item.astype(BF16) for item in bases[0] + bases[1][1:]], marks
    )
    steps = order[outer // 2 :] + order[1 : outer // 2]
    arrived = [push(item, devices, 0, k) for item, k in zip(sent, steps)]
    return total(bases[1][0], *arrived), marks


def order_bases(bases, marks):
    values, marks = order_after(bases[0] + bases[1], marks)
    half = len(bases[0])
    return [values[:half], values[half:]], marks


def tree_sizes(devices):
    outer = devices // 4
    return [outer // 2] * 6 + [outer // 4] * 4


def small_split(value):
    count = value.shape[0] // 4
    half = count // 2
    cuts = (0, count, 2 * count, 3 * count, 3 * count + half, 4 * count)
    return [value[a:b] for a, b in zip(cuts, cuts[1:])]


LIMIT = 58 * 1024 * 1024


def mm(left, right):
    return jnp.dot(left, right, preferred_element_type=F32)


def mm_t(left, right):
    return lax.dot_general(left, right, (((1,), (1,)), ((), ())), preferred_element_type=F32)


def t_mm(left, right):
    return lax.dot_general(left, right, (((0,), (0,)), ((), ())), preferred_element_type=F32)


TREE = 10


def call(kernel, out_shape, places, scratch, flops, moved, *args, outs=None, aliases=None, marks=()):
    count = len(args)

    def without_marks(*refs):
        kernel(*refs[:count], *refs[count + len(marks) :])

    outs = outs or [pltpu.VMEM] * len(out_shape)
    places = list(places) + [pl.ANY] * len(marks)
    return pl.pallas_call(
        without_marks,
        out_shape=out_shape,
        in_specs=[pl.BlockSpec(memory_space=place) for place in places],
        out_specs=tuple(pl.BlockSpec(memory_space=place) for place in outs),
        input_output_aliases=aliases or {},
        scratch_shapes=scratch,
        compiler_params=pltpu.CompilerParams(vmem_limit_bytes=LIMIT),
        cost_estimate=pl.CostEstimate(flops=flops, bytes_accessed=moved, transcendentals=0),
    )(*args, *marks)


def sds(shape, dtype=BF16):
    return jax.ShapeDtypeStruct(shape, dtype)


def tree_copies(pieces, whole, sems, m, out=False):
    tok = whole.shape[1]
    copies, at = [], 0
    for place, piece in enumerate(pieces):
        count = piece.shape[0]
        ends = piece.at[:, pl.ds(m * tok, tok)], whole.at[pl.ds(at, count)]
        if out:
            ends = ends[::-1]
        copies.append(pltpu.make_async_copy(*ends, sems.at[place]))
        at += count
    return copies


def run(copies):
    for copy in copies:
        copy.start()
    for copy in copies:
        copy.wait()


def rows_of(whole, start, count):
    value = whole[pl.ds(start, count)]
    return value.reshape(count * value.shape[1], value.shape[2])


def attend_kernel(
    order, length, *refs,
):
    pieces = refs[:TREE]
    (query_w, latent_w, expand_w, gain, latent_gain, turn, pos_q, pos_k,
     out, q_nope, q_rot, k_nope, k_rot, val, latent_n, probs, factor, latent_own,
     x, sems) = refs[TREE:]
    blocks, tok, width = x.shape
    quarter = blocks // 4
    span = quarter * tok
    scale = (DN + DR) ** (-0.5)
    lane = lax.broadcasted_iota(jnp.int32, (1, 128), 1)
    loads = [tree_copies(pieces, x, sems, m) for m in range(MICRO)]
    for copy in loads[0]:
        copy.start()
    for m in range(MICRO):
        for copy in loads[m]:
            copy.wait()

        @pl.loop(0, 4, unroll=2)
        def _(g):
            here = pl.ds(pl.multiple_of(g * span, span), span)
            value = rows_of(x, g * quarter, quarter).astype(F32)
            inv = lax.rsqrt(jnp.mean(value * value, axis=-1, keepdims=True) + EPS)
            factor[m, here, :] = inv
            normed = (value * inv * gain[...]).astype(BF16)
            query = mm(normed, query_w[...])
            mixed = mm(normed, latent_w[...])
            latent = mixed[:, :R]

            @pl.when(g == 0)
            def _():
                latent_own[m] = latent[:tok]

            inv_l = lax.rsqrt(jnp.mean(latent * latent, axis=-1, keepdims=True) + EPS)
            low = (latent * inv_l * latent_gain[...]).astype(BF16)
            latent_n[m, here, :] = low
            q_nope[m, here, :] = query[:, :DN].astype(BF16)
            turned = query[:, DN:] * turn[here, :]
            q_rot[m, here, :] = (turned + pltpu.roll(turned, DR, 1)).astype(BF16)
            turned = mixed[:, R:] * turn[here, :]
            k_rot[m, here, :] = (turned + pltpu.roll(turned, DR, 1)).astype(BF16)
            kv = mm(low, expand_w[...])
            k_nope[m, here, :] = kv[:, :DN].astype(BF16)
            val[m, here, :] = kv[:, DN:].astype(BF16)

        if m + 1 < MICRO:
            for copy in loads[m + 1]:
                copy.start()
        half_k = jnp.where(lane < DR, k_rot[m], jnp.zeros_like(k_rot[m]))

        @pl.loop(0, 4, unroll=2)
        def _(g):
            here = pl.ds(pl.multiple_of(g * span, span), span)
            scores = mm_t(q_nope[m, here, :], k_nope[m]) + mm_t(q_rot[m, here, :], half_k)
            visible = (pos_k[...] <= pos_q[here, :]) & (pos_k[...] < length[m])
            scores = jnp.where(visible, scores * scale, -1e30)
            raised = jnp.exp(scores - jnp.max(scores, axis=-1, keepdims=True))
            prob = (raised / jnp.sum(raised, axis=-1, keepdims=True)).astype(BF16)
            probs[m, here, :] = prob
            value = mm(prob, val[m]).astype(BF16).reshape(quarter, tok, DV)
            for i in range(quarter):
                out[order[g * quarter + i], pl.ds(m * tok, tok), :] = value[i]


def attend(order, length, pieces, query_w, latent_w, expand_w, gain, latent_gain, turn, pos):
    blocks = sum(piece.shape[0] for piece in pieces)
    tok, width = pieces[0].shape[1] // MICRO, query_w.shape[0]
    seq = blocks * tok
    small = sds((MICRO, seq, 128))
    return call(
        attend_kernel,
        (sds((blocks, MICRO * tok, DV)), small, small, small, small, small,
         sds((MICRO, seq, R)), sds((MICRO, seq, seq)), sds((MICRO, seq, 1), F32),
         sds((MICRO, tok, R), F32)),
        [pltpu.SMEM] * 2 + [pl.ANY] * TREE + [pltpu.VMEM] * 8,
        [pltpu.VMEM((blocks, tok, width), BF16), pltpu.SemaphoreType.DMA((TREE,))],
        2 * MICRO * seq * (width * 896 + R * 256 + seq * 384),
        2 * MICRO * seq * (width + seq + 1200) + 1800 * width,
        order, length, *pieces, query_w, latent_w, expand_w, gain.reshape(1, -1),
        latent_gain.reshape(1, -1), turn, pos.reshape(seq, 1), pos.reshape(1, seq),
    )


def attend_back_kernel(order, *refs):
    pieces = refs[:TREE]
    (grad, q_nope, q_rot, k_nope, k_rot, val, latent_n, probs, factor, query_w, expand_w, gain,
     turn) = refs[TREE : TREE + 13]
    (grad_queries, l0, l1, l2, l3, l4, grad_query_w, grad_expand_w, part,
     x, prob_all, grad_k, grad_r, grad_v, sems, prob_sem) = refs[TREE + 13 :]
    blocks, tok, width = x.shape
    quarter = blocks // 4
    span = quarter * tok
    scale = (DN + DR) ** (-0.5)
    grad_query_w[...] = jnp.zeros_like(grad_query_w)
    part[...] = jnp.zeros_like(part)
    lane = lax.broadcasted_iota(jnp.int32, (1, 128), 1)
    for m in range(MICRO):
        load = pltpu.make_async_copy(probs.at[m], prob_all, prob_sem)
        run(tree_copies(pieces, x, sems, m) + [load])
        grad_k[...] = jnp.zeros_like(grad_k)
        grad_r[...] = jnp.zeros_like(grad_r)
        grad_v[...] = jnp.zeros_like(grad_v)

        @pl.loop(0, 4, unroll=2)
        def _(g):
            here = pl.ds(pl.multiple_of(g * span, span), span)
            above = jnp.concatenate(
                [grad[order[g * quarter + i], pl.ds(m * tok, tok), :] for i in range(quarter)],
                axis=0,
            )
            prob_low = prob_all[here, :]
            prob = prob_low.astype(F32)
            weighted = prob * mm_t(above, val[m])
            slope = (weighted - prob * jnp.sum(weighted, axis=-1, keepdims=True)).astype(BF16)
            grad_k[...] += t_mm(slope, q_nope[m, here, :])
            grad_r[...] += t_mm(slope, q_rot[m, here, :])
            grad_v[...] += t_mm(prob_low, above)
            nope = (mm(slope, k_nope[m]) * scale).astype(BF16)
            turned = mm(slope, k_rot[m]) * (scale * turn[here, :])
            grad_q = jnp.concatenate([nope, turned.astype(BF16)], axis=1)
            back = jnp.where(
                lane < DR // 2,
                turned + pltpu.roll(turned, DR // 2, 1),
                turned - pltpu.roll(turned, 128 - DR // 2, 1),
            )
            both = jnp.concatenate([nope, back.astype(BF16)], axis=1).reshape(quarter, tok, 256)
            for i in range(quarter):
                grad_queries[order[g * quarter + i], pl.ds(m * tok, tok), :] = both[i]
            value = rows_of(x, g * quarter, quarter).astype(F32) * factor[m, here, :]
            grad_query_w[...] += t_mm((value * gain[...]).astype(BF16), grad_q)
            normed = mm_t(grad_q, query_w[...])
            part[...] += jnp.sum(normed * value, axis=0, keepdims=True)

        grad_kv = jnp.concatenate([grad_k[...] * scale, grad_v[...]], axis=1).astype(BF16)
        expand_sum = t_mm(latent_n[m], grad_kv)
        grad_expand_w[...] = expand_sum if m == 0 else grad_expand_w[...] + expand_sum
        latent = jnp.concatenate(
            [mm_t(grad_kv, expand_w[...]).astype(BF16), (grad_r[...] * scale).astype(BF16)], axis=1
        ).reshape(blocks, tok, R + 128)
        at = 0
        for ref in (l0, l1, l2, l3, l4):
            count = ref.shape[0]
            ref[:, pl.ds(m * tok, tok), :] = latent[at : at + count]
            at += count


def attend_back(order, pieces, grad, saved, query_w, expand_w, gain, turn, marks):
    blocks = sum(piece.shape[0] for piece in pieces)
    both, width = pieces[0].shape[1], query_w.shape[0]
    tok = both // MICRO
    seq = blocks * tok
    quarter = blocks // 4
    sizes = (quarter,) * 3 + (quarter // 2,) * 2
    return call(
        attend_back_kernel,
        (sds((blocks, both, 256)),)
        + tuple(sds((count, both, R + 128)) for count in sizes)
        + (sds((width, 256), F32), sds((R, 256), F32), sds((1, width), F32)),
        [pltpu.SMEM] + [pl.ANY] * TREE + [pltpu.VMEM] * 7 + [pl.ANY] + [pltpu.VMEM] * 5,
        [pltpu.VMEM((blocks, tok, width), BF16), pltpu.VMEM((seq, seq), BF16)]
        + [pltpu.VMEM((seq, 128), F32)] * 3
        + [pltpu.SemaphoreType.DMA((TREE,)), pltpu.SemaphoreType.DMA],
        2 * MICRO * seq * (width * 512 + R * 512 + seq * 768),
        2 * MICRO * seq * (2 * width + seq + 2000) + 2 * query_w.size,
        order, *pieces, grad, *saved[1:9], query_w, expand_w, gain.reshape(1, -1), turn,
        marks=marks,
    )


def early_kernel(m, *refs):
    pieces = refs[:TREE]
    pick, row_gate, down, shared_down, back, grad_eh, grad_shared, whole, g, sems = refs[TREE:]
    blocks, tok, width = g.shape
    quarter = blocks // 4
    room = pick.shape[1]
    run(tree_copies(pieces, g, sems, m))

    @pl.loop(0, 4)
    def _(q):
        value = rows_of(g, q * quarter, quarter)
        here = pl.ds(pl.multiple_of(q * room, room), room)
        back[here, :] = (row_gate[here, :] * mm(pick[q], value)).astype(BF16)
        span = quarter * tok
        there = pl.ds(pl.multiple_of(q * span, span), span)
        grad_shared[there, :] = mm_t(value, shared_down[...])
        whole[there, :] = value

    total_rows = down.shape[0]
    for start in range(0, total_rows, 512):
        here = pl.ds(start, min(512, total_rows - start))
        grad_eh[:, here] = mm_t(back[...], down[here, :])


def early(m, pieces, pick, row_gate, down, shared_down, marks):
    blocks = sum(piece.shape[0] for piece in pieces)
    tok, width = pieces[0].shape[1] // MICRO, down.shape[1]
    rows, units = pick.shape[0] * pick.shape[1], shared_down.shape[0]
    return call(
        functools.partial(early_kernel, m),
        (sds((rows, width)), sds((rows, down.shape[0]), F32), sds((blocks * tok, units), F32),
         sds((blocks * tok, width))),
        [pl.ANY] * TREE + [pltpu.VMEM] * 4,
        [pltpu.VMEM((blocks, tok, width), BF16), pltpu.SemaphoreType.DMA((TREE,))],
        2 * rows * width * (down.shape[0] + 256),
        2 * width * (2 * blocks * tok + rows + down.shape[0]) + 4 * rows * down.shape[0],
        *pieces, pick, row_gate, down, shared_down, marks=marks,
    )


def expert_kernel(m, *refs):
    pieces = refs[:TREE]
    pick, grad_eh, grad_shared, both, share_g, share_u = refs[TREE : TREE + 6]
    first = TREE + 6 + (TREE if m else 0)
    mixed, arrived, hidden, grad_gu, shared_hidden, grad_sg, grad_su = refs[first : first + 7]
    outs = refs[first + 7 : first + 7 + TREE]
    x, w, o, sems, w_sems = refs[first + 7 + TREE :]
    blocks, tok, width = x.shape
    quarter = blocks // 4
    span = quarter * tok
    room = pick.shape[1]
    chunks = w.shape[0] // 256
    copies = tree_copies(pieces, x, sems, m)
    for copy in copies:
        copy.start()
    loads = [
        pltpu.make_async_copy(both.at[pl.ds(f * 256, 256)], w.at[pl.ds(f * 256, 256)], w_sems.at[f])
        for f in range(chunks)
    ]
    for copy in loads:
        copy.start()
    for copy in copies:
        copy.wait()

    @pl.loop(0, 4)
    def _(q):
        value = rows_of(x, q * quarter, quarter)
        there = pl.ds(pl.multiple_of(q * span, span), span)
        here = pl.ds(pl.multiple_of(q * room, room), room)
        mixed[there, :] = value
        arrived[here, :] = mm(pick[q], value).astype(BF16)
        gate = mm(value, share_g[...])
        lift = mm(value, share_u[...])
        sigma = 1.0 / (1.0 + jnp.exp(-gate))
        grad = grad_shared[there, :]
        shared_hidden[there, :] = (gate * sigma * lift).astype(BF16)
        grad_sg[there, :] = (grad * lift * sigma * (1.0 + gate * (1.0 - sigma))).astype(BF16)
        grad_su[there, :] = (grad * gate * sigma).astype(BF16)

    for copy in loads:
        copy.wait()

    def units(start, count):
        value = mm_t(arrived[...], w[pl.ds(start, count * 256), :])
        for j in range(count):
            at = pl.multiple_of(start + j * 256, 256)
            half = pl.multiple_of(start // 2 + j * 128, 128)
            gate = value[:, j * 256 : j * 256 + 128]
            lift = value[:, j * 256 + 128 : (j + 1) * 256]
            sigma = 1.0 / (1.0 + jnp.exp(-gate))
            grad = grad_eh[:, pl.ds(half, 128)]
            hidden[:, pl.ds(half, 128)] = (gate * sigma * lift).astype(BF16)
            grad_gu[:, pl.ds(at, 128)] = (
                grad * lift * sigma * (1.0 + gate * (1.0 - sigma))
            ).astype(BF16)
            grad_gu[:, pl.ds(pl.multiple_of(at + 128, 128), 128)] = (grad * gate * sigma).astype(BF16)

    @pl.loop(0, chunks // 2)
    def _(f):
        units(pl.multiple_of(f * 512, 512), 2)

    if chunks % 2:
        units((chunks - 1) * 256, 1)

    spread_out(
        o, pick, 512,
        lambda cols: mm(grad_gu[...], w[:, cols]).astype(BF16),
        lambda there, cols: mm_t(grad_sg[there, :], share_g[cols, :])
        + mm_t(grad_su[there, :], share_u[cols, :]),
    )
    run(tree_copies(outs, o, sems, m, True))


def spread_out(o, pick, step, routed, shared):
    blocks, tok, width = o.shape
    quarter = blocks // 4
    span = quarter * tok
    room = pick.shape[1]

    @pl.loop(0, width // step)
    def _(c):
        cols = pl.ds(pl.multiple_of(c * step, step), step)
        value = routed(cols)
        for q in range(4):
            there = pl.ds(q * span, span)
            tokens = t_mm(pick[q], value[q * room : (q + 1) * room]) + shared(there, cols)
            o[pl.ds(q * quarter, quarter), :, cols] = tokens.astype(BF16).reshape(
                quarter, tok, step
            )


def experts(m, pieces, pick, grad_eh, grad_shared, both, share_g, share_u, earlier):
    blocks = sum(piece.shape[0] for piece in pieces)
    tok, width = pieces[0].shape[1] // MICRO, pieces[0].shape[2]
    seq, rows, units = blocks * tok, pick.shape[0] * pick.shape[1], share_g.shape[1]
    hid = both.shape[0] // 2
    whole = pltpu.VMEM((blocks, tok, width), BF16)
    return call(
        functools.partial(expert_kernel, m),
        (sds((seq, width)), sds((rows, width)), sds((rows, hid)), sds((rows, 2 * hid)))
        + (sds((seq, units)),) * 3 + tuple(sds(piece.shape) for piece in pieces),
        [pl.ANY] * TREE + [pltpu.VMEM] * 3 + [pl.ANY] + [pltpu.VMEM] * 2
        + [pl.ANY] * len(earlier),
        [whole, pltpu.VMEM(both.shape, BF16), whole,
         pltpu.SemaphoreType.DMA((TREE,)), pltpu.SemaphoreType.DMA((both.shape[0] // 256,))],
        8 * rows * width * hid + 8 * seq * width * 256,
        2 * both.size + 6 * seq * width + 10 * rows * hid,
        *pieces, pick, grad_eh, grad_shared, both, share_g, share_u, *earlier,
        outs=[pltpu.VMEM] * 7 + [pl.ANY] * TREE,
        aliases={TREE + 6 + i: 7 + i for i in range(len(earlier))},
    )


def output_kernel(m, *refs):
    hidden, row_gate, pick, down, shared_hidden, shared_down = refs[:6]
    first = 6 + (TREE if m else 0)
    outs = refs[first : first + TREE]
    o, sems = refs[first + TREE :]
    spread_out(
        o, pick, 512,
        lambda cols: (
            row_gate[...] * mm(hidden[...], down[:, cols]).astype(BF16).astype(F32)
        ).astype(BF16),
        lambda there, cols: mm(shared_hidden[there, :], shared_down[:, cols]),
    )
    run(tree_copies(outs, o, sems, m, True))


def expert_output(m, pieces, hidden, row_gate, pick, down, shared_hidden, shared_down, earlier,
                  marks):
    blocks = sum(piece.shape[0] for piece in pieces)
    tok, width = pieces[0].shape[1] // MICRO, pieces[0].shape[2]
    return call(
        functools.partial(output_kernel, m),
        tuple(sds(piece.shape) for piece in pieces),
        [pltpu.VMEM] * 6 + [pl.ANY] * len(earlier),
        [pltpu.VMEM((blocks, tok, width), BF16), pltpu.SemaphoreType.DMA((TREE,))],
        2 * hidden.size * width + 4 * blocks * tok * 256 * width,
        2 * down.size + 2 * hidden.size + 2 * blocks * tok * width,
        hidden, row_gate, pick, down, shared_hidden, shared_down, *earlier,
        marks=marks,
        outs=[pl.ANY] * TREE,
        aliases={6 + i: i for i in range(len(earlier))},
    )


def weight_kernel(reps, count, *refs):
    l0, l1, r0, r1, *outs = refs[count:]
    unit = 128 // reps
    value = t_mm(l0[...], r0[...]) + t_mm(l1[...], r1[...])
    for index, ref in enumerate(outs):
        for part in range(reps):
            start = index * 128 + part * unit
            ref[part] = value[start : start + unit].astype(ref.dtype)


def weight_sums(reps, lanes, left, right, marks):
    rows, width = right[0].shape
    hid = left[0].shape[1] * 128 // lanes
    chunks, unit = hid // 128, 128 // reps
    whole = pl.BlockSpec((rows, width), lambda f: (0, 0), pipeline_mode=pl.Buffered(1))
    part = pl.BlockSpec((reps, unit, width), lambda f: (0, f, 0))
    return pl.pallas_call(
        functools.partial(weight_kernel, reps, len(marks)),
        grid=(chunks,),
        in_specs=[pl.BlockSpec(memory_space=pl.ANY)] * len(marks)
        + [pl.BlockSpec((rows, lanes), lambda f: (0, f))] * 2 + [whole] * 2,
        out_specs=[part] * (lanes // 128),
        out_shape=[sds((reps, hid // reps, width))] * (lanes // 128),
        compiler_params=pltpu.CompilerParams(vmem_limit_bytes=LIMIT),
        cost_estimate=pl.CostEstimate(
            flops=4 * rows * width * hid * lanes // 128,
            bytes_accessed=10 * width * hid,
            transcendentals=0,
        ),
    )(*marks, *left, *right)


def rep_pull(value, count, step):
    return lax.ppermute(value, "rep", [((d + step) % count, d) for d in range(count)])


def rep_parts(value, count):
    return [value] + [rep_pull(value, count, step) for step in range(1, count)]


def rep_total(parts, count):
    value = parts[0].astype(F32)
    for step in range(1, count):
        perm = [(d, (d + step) % count) for d in range(count)]
        value = value + lax.ppermute(parts[step], "rep", perm).astype(F32)
    return value


def rep_sum(value):
    return jnp.sum(lax.all_gather(value.astype(BF16), "rep", axis=0).astype(F32), axis=0)


def body(
    hidden_in,
    cotangent,
    lengths,
    routes,
    gate_values,
    attn_gain,
    query_proj,
    latent_proj,
    latent_gain,
    expand_proj,
    output_proj,
    ffn_gain,
    shared_gate,
    shared_lift,
    shared_down,
    expert_gate,
    expert_lift,
    expert_down,
):
    tok = hidden_in.shape[1]
    width = hidden_in.shape[2]
    n = lax.axis_size("fsdp")
    reps = lax.axis_size("rep")
    me = lax.axis_index("fsdp")
    rep = lax.axis_index("rep")
    outer = n // 4
    seq = tok * n
    capacity = min(tok, 3 * tok * TOP // (2 * n))
    split = max(1, n // H)
    rows = width // n

    slots = jnp.arange(n, dtype=jnp.int32)
    nearness = near_first(outer)
    steps_on = jnp.asarray(nearness, jnp.int32)
    place_of = jnp.asarray([nearness.index(k) for k in range(outer)], jnp.int32)
    abs_of_rel = ((me // 4 + steps_on[slots % outer]) % outer) * 4 + ((me % 4) ^ (slots // outer))
    rel_of_abs = ((slots % 4) ^ (me % 4)) * outer + place_of[(slots // 4 - me // 4) % outer]
    rep_order = (jnp.arange(reps, dtype=jnp.int32) - rep) % reps
    own_pos = me * tok + jnp.arange(tok, dtype=jnp.int32)
    pos = (abs_of_rel[:, None] * tok + jnp.arange(tok, dtype=jnp.int32)[None, :]).reshape(seq)
    freqs = THETA ** (-(2.0 * jnp.arange(DR // 2, dtype=F32)) / DR)
    angles = pos.astype(F32)[:, None] * freqs[None, :]
    cosine, sine = jnp.cos(angles), jnp.sin(angles)
    turn = jnp.concatenate([cosine, cosine, sine, sine], axis=1)

    def all_to_all(value):
        return lax.all_to_all(value, "fsdp", split_axis=0, concat_axis=0, tiled=True)

    def rep_slice(value, axis):
        size = value.shape[axis] // reps
        return lax.dynamic_slice_in_dim(value, rep * size, size, axis)

    def rep_join(value, axis):
        parts = jnp.take(jnp.stack(rep_parts(value, reps)), rep_order, axis=0)
        return jnp.concatenate([parts[i] for i in range(reps)], axis=axis)

    def unreshard(value):
        return rep_sum(all_to_all(value.astype(BF16)))

    def by_head(value):
        return jnp.repeat(value, split, axis=0) if split > 1 else value

    both = MICRO * tok
    dense_gate = jnp.sum(
        jnp.where(routes[..., None] == slots, gate_values[..., None], 0.0), axis=2
    ).reshape(both, n)
    gate_high = dense_gate.astype(BF16)
    gate_low = (dense_gate - gate_high.astype(F32)).astype(BF16)

    def fit(value):
        return jnp.pad(value, ((0, both - value.shape[0]), (0, 0)))

    items = [
        fit(latent_proj),
        gate_high,
        gate_low,
        fit(attn_gain[:, None]),
        fit(ffn_gain[:, None]),
        fit(latent_gain[:, None]),
    ]
    starts = [0]
    for item in items:
        starts.append(starts[-1] + item.shape[1])
    fill = jnp.zeros((both, -starts[-1] % 128), BF16)
    small = gather_small("small", jnp.concatenate(items + [fill], axis=1), n)[0]
    extras = jnp.concatenate(small, axis=0)
    latent_w = jnp.take(extras[:, :rows, : starts[1]], rel_of_abs, axis=0).reshape(width, R + DR)
    gates = extras[..., starts[1] : starts[3]].reshape(n, both, 2, n).astype(F32)
    gates = jnp.sum(jnp.where(slots == me, gates, 0.0), axis=(2, 3))
    gains = jnp.take(extras[..., starts[3] : starts[6]], rel_of_abs, axis=0).astype(F32)
    gains = jnp.transpose(gains, (2, 0, 1))
    attn_gain_f = gains[0, :, :rows].reshape(width)
    ffn_gain_f = gains[1, :, :rows].reshape(width)
    latent_gain_f = gains[2, :, : R // n].reshape(R)

    head_w = jnp.concatenate(
        [
            jnp.transpose(query_proj.reshape(rows, H, DN + DR), (1, 0, 2)),
            jnp.transpose(expand_proj.reshape(R // n, H, DN + DV), (1, 0, 2)).reshape(
                H, rows, -1
            ),
        ],
        axis=2,
    )
    head_w = all_to_all(by_head(head_w))
    query_w = head_w[..., : DN + DR].reshape(width, DN + DR)
    expand_w = head_w[..., DN + DR :].reshape(R, DN + DV)
    query_w = jnp.concatenate([query_w] + swapped(query_w[:, DN:]), axis=1)
    latent_in = jnp.concatenate([latent_w] + swapped(latent_w[:, R:]), axis=1)

    unit = 128 // reps

    def chunked(*weights):
        parts = [lax.all_gather(item, "rep", axis=0) for item in weights]
        return jnp.stack(
            [part[i].reshape(-1, unit, width) for part in parts for i in range(reps)], axis=1
        ).reshape(-1, width)

    both_w = chunked(jnp.swapaxes(expert_gate[0], 0, 1), jnp.swapaxes(expert_lift[0], 0, 1))
    down_w = chunked(expert_down[0])
    block = hidden_in.reshape(both, width)
    hidden_all, given = gather_tree(
        "hidden", block, n, ((), (), [query_w, latent_in, expand_w, both_w, down_w])
    )
    query_w, latent_in, expand_w, both_w, down_w = given[2]

    cols = width // reps
    used = (own_pos[None, :] < lengths[:, None])[..., None]
    grad_rows = jnp.where(used, cotangent, jnp.zeros_like(cotangent)).reshape(both, width)
    (out_share,), hidden_all[1:2] = order_after([rep_slice(output_proj, 1)], hidden_all[1:2])
    out_marks = hidden_all[3:4]
    att = attend(
        abs_of_rel, lengths, hidden_all, query_w, latent_in, expand_w,
        attn_gain_f, latent_gain_f, turn, pos,
    )
    att = list(att)

    out_pieces, _, att[0:1] = gather_small("output_w", out_share, n, out_marks, att[0:1])
    heads_out = all_to_all(att[0])
    (grad_rows,), out_pieces[0:1] = order_after([grad_rows], out_pieces[0:1])
    grad_all, given = gather_tree("cotangent", grad_rows, n, (out_pieces[1:3] + [heads_out], (), ()))
    out_pieces[1], out_pieces[2], heads_out = given[0]
    heads_out = heads_out[::split]
    heads_local = jnp.transpose(heads_out, (1, 0, 2)).reshape(both, n, H * DV // n)
    heads_local = jnp.take(heads_local, abs_of_rel, axis=1).reshape(both, H * DV)
    cols = width // reps
    out_w = rep_parts(jnp.concatenate(out_pieces, axis=0).reshape(H * DV, cols), reps)

    def columns(step):
        return ((rep + step) % reps) * cols

    merge = 1
    while (merge * capacity) % 16:
        merge *= 2
    groups = n // merge
    span = merge * tok
    room = merge * capacity
    upper = (jnp.arange(span)[:, None] <= jnp.arange(span)[None, :]).astype(BF16)

    hidden = hidden_in.reshape(both, width).astype(F32)
    residual = jnp.zeros((both, width), F32)
    for step in range(reps):
        share = contract("tj,jd->td", heads_local, out_w[step])
        residual = lax.dynamic_update_slice(residual, share, (0, columns(step)))
    residual = hidden + residual
    mixed, inv_second = rms_forward(residual, ffn_gain_f)
    mixed = mixed.astype(BF16)
    (shared_gate, shared_lift), (mixed,) = order_after([shared_gate, shared_lift], [mixed])

    ahead = []
    for m in range(MICRO):
        gate_here = gates[:, m * tok : (m + 1) * tok].reshape(groups, span)
        hit = gate_here > 0.0
        place = contract("gt,ts->gs", hit.astype(BF16), upper).astype(jnp.int32) - 1
        chosen = hit[:, None, :] & (
            place[:, None, :] == jnp.arange(room, dtype=jnp.int32)[None, :, None]
        )
        pick = chosen.astype(BF16)
        row_gate = jnp.sum(jnp.where(chosen, gate_here[:, None, :], 0.0), axis=2).reshape(-1, 1)
        ahead.append(
            (pick, row_gate) + early(m, grad_all, pick, row_gate, down_w, shared_down,
                    (ahead[0][2],) if m else (mixed,))
        )

    shared_in = jnp.concatenate(
        [
            jnp.transpose(shared_gate.reshape(rows, n, -1), (1, 0, 2)),
            jnp.transpose(shared_lift.reshape(rows, n, -1), (1, 0, 2)),
        ],
        axis=2,
    )
    units = shared_in.shape[2] // 2
    shared_in = all_to_all(shared_in)
    marks = [list(item) for item in ahead]
    mixed_all, given = gather_tree(
        "mixed", mixed, n, ((), [marks[0][2], shared_in, both_w], [marks[1][2]])
    )
    marks[0][2], shared_in, both_w = given[1]
    marks[1][2:3] = given[2]
    shared_in = shared_in.reshape(width, 2 * units)
    ahead = marks

    share_g, share_u = shared_in[:, :units], shared_in[:, units:]

    share = jnp.concatenate([rep_slice(query_proj, 1)], axis=1)
    (share,), mixed_all[8:] = order_after([share], mixed_all[8:])
    whole_query = lax.all_gather(share, "fsdp", axis=0, tiled=True)

    done = []
    earlier = ()
    for m in range(MICRO):
        pick, row_gate, back, grad_eh, grad_shared, _ = ahead[m]
        done.append(
            experts(m, mixed_all, pick, grad_eh, grad_shared, both_w, share_g, share_u, earlier)
        )
        earlier = done[m][7:]
    earlier = list(earlier)
    pieces = ()
    halves = scatter_tree_last("grad_mixed", earlier, n)
    bases = scatter_tree_cross("grad_mixed", halves, n)
    stages = [(halves[0][1],), (halves[1][2],), (bases[0][0],), (bases[1][0],)]
    for m in range(MICRO):
        pick, row_gate = ahead[m][:2]
        pieces = list(
            expert_output(
                m, mixed_all, done[m][2], row_gate, pick, down_w, done[m][4], shared_down,
                pieces, stages[2 * m],
            )
        )
        if m == 0:
            down_sums = list(
                weight_sums(
                    reps, 128, (done[0][2], done[1][2]), (ahead[0][2], ahead[1][2]),
                    stages[1] + (pieces[0],),
                )
            )
            share_grads, down_sums[0:1] = order_after(
                [done[0][5], done[1][5]], list(down_sums[0:1])
            )
            stages[2] += (down_sums[0],)
    down_sums = list(down_sums)
    both_sums = weight_sums(
        reps, 256, (done[0][3], done[1][3]), (done[0][1], done[1][1]),
        stages[3] + (pieces[0],),
    )
    both_sums = list(both_sums)
    grad_mixed, _ = scatter_tree_rest("grad_mixed", bases, n)
    grad_shared_in = sum(
        contract("td,tf->df", done[m][0], jnp.concatenate([share_grads[m], done[m][6]], axis=1))
        for m in range(MICRO)
    )
    grad_shared_in = all_to_all(grad_shared_in.astype(BF16).reshape(n, rows, 2 * units))
    (grad_mixed,), (both_sums[0], grad_shared_in) = order_after(
        [grad_mixed], [both_sums[0], grad_shared_in]
    )
    whole_query = lax.all_gather(whole_query, "rep", axis=0)
    expert_sums = [
        lax.psum_scatter(item, "rep", scatter_dimension=0) for item in both_sums + down_sums
    ]
    grad_res, part_ffn = rms_backward(residual, inv_second, ffn_gain_f, grad_mixed)
    grad_res = grad_res + grad_rows.astype(F32)
    grad_res_low = grad_res.astype(BF16)
    grad_heads = sum(
        contract(
            "td,jd->tj",
            lax.dynamic_slice_in_dim(grad_res_low, columns(step), cols, 1),
            out_w[step],
        )
        for step in range(reps)
    )
    grad_heads = jnp.take(
        grad_heads.astype(BF16).reshape(both, n, H * DV // n), rel_of_abs, axis=1
    )
    grad_heads = jnp.transpose(grad_heads.reshape(both, H, DV), (1, 0, 2))
    grad_heads = by_head(grad_heads)
    grad_heads = all_to_all(grad_heads)
    if split > 1:
        grad_heads = jnp.where(me % split == 0, grad_heads, jnp.zeros_like(grad_heads))

    shares = []
    for step in range(reps):
        piece = lax.dynamic_slice_in_dim(grad_res_low, columns(step), cols, 1)
        shares.append(contract("tj,td->jd", heads_local, piece))
    out_total = rep_total([shares[0]] + [item.astype(BF16) for item in shares[1:]], reps)
    out_total = out_total.astype(BF16).reshape(n, rows, cols)
    out_pieces = small_split(out_total)

    result = attend_back(
        abs_of_rel, hidden_all, grad_heads, att, query_w, expand_w, attn_gain_f, turn,
        [whole_query] + expert_sums,
    )
    result = list(result)
    pieces[6:], result[6:7] = order_after(pieces[6:], result[6:7])
    halves = scatter_tree_last("routed", pieces, n)
    expert_sums, result[1:2] = order_after(expert_sums, result[1:2])
    grad_expert_gate, grad_expert_lift, grad_expert_down = [
        item.astype(F32) for item in expert_sums
    ]
    (grad_shared_in,), result[2:3] = order_after([grad_shared_in], result[2:3])
    grad_shared_in = rep_sum(grad_shared_in)
    grad_shared_gate = jnp.transpose(grad_shared_in[:, :, :units], (1, 0, 2)).reshape(rows, -1)
    grad_shared_lift = jnp.transpose(grad_shared_in[:, :, units:], (1, 0, 2)).reshape(rows, -1)
    down_sum = sum(contract("tf,td->fd", done[m][4], ahead[m][5]) for m in range(MICRO))
    grad_shared_down = rep_sum(down_sum)


    bases = scatter_tree_cross("routed", halves, n)
    grad_queries = all_to_all(result[0])
    grad_latent = scatter_small_last("grad_latent", result[1:6], n)
    grad_latent, (grad_queries,) = scatter_small_rest(
        "grad_latent", grad_latent, n, [grad_queries]
    )
    routed, (grad_latent,) = scatter_tree_rest("routed", bases, n, [grad_latent])
    outputs = (residual + routed).astype(BF16).reshape(MICRO, tok, width)
    out_pieces[3:], (grad_latent,) = order_after(out_pieces[3:], [grad_latent])
    out_pieces = scatter_small_last("grad_output_w", out_pieces, n)
    grad_q, grad_expand_w, part_attn = result[6:]

    latent = att[9].reshape(both, R)
    inv = lax.rsqrt(jnp.mean(latent * latent, axis=-1, keepdims=True) + EPS)
    grad_c, part_latent = rms_backward(latent, inv, latent_gain_f, grad_latent[:, :R])
    own_cos, own_sin = jnp.tile(cosine[:tok], (MICRO, 1)), jnp.tile(sine[:tok], (MICRO, 1))
    grad_krope = rotate_back(grad_latent[:, R : R + DR], own_cos, own_sin)
    grad_kva = jnp.concatenate([grad_c, grad_krope], axis=1).astype(BF16)
    grad_local = contract("tj,dj->td", grad_kva, latent_w)
    factor = att[8][:, :tok].reshape(both, 1)
    part_attn = part_attn[0] + jnp.sum(grad_local * hidden * factor, axis=0)

    gain_parts = jnp.stack(
        [
            part_attn.reshape(n, rows),
            part_ffn.reshape(n, rows),
            jnp.pad(part_latent.reshape(n, R // n), ((0, 0), (0, rows - R // n))),
        ],
        axis=1,
    )
    kv_pieces = gather_small("grad_kv", grad_kva, n)[0]

    turn_part = grad_q[:, DN + DR :]
    half = DR // 2
    grad_q = jnp.concatenate(
        [
            grad_q[:, :DN],
            grad_q[:, DN : DN + half] + turn_part[:, half:],
            grad_q[:, DN + half : DN + DR] - turn_part[:, :half],
        ],
        axis=1,
    )
    head_grad = jnp.concatenate(
        [grad_q.reshape(n, rows, DN + DR), grad_expand_w.reshape(n, rows, -1)], axis=2
    ).astype(BF16)
    gain_high = gain_parts.astype(BF16)
    gain_low = (gain_parts - gain_high.astype(F32)).astype(BF16)
    gain_rows = jnp.stack([gain_high, gain_low], axis=1).reshape(n, -1)
    gain_count = gain_rows.shape[1]
    head_cols = head_grad.shape[2]
    gain_rows = jnp.pad(gain_rows, ((0, 0), (0, 16 * head_cols - gain_count)))
    head_grad = jnp.concatenate([head_grad, gain_rows.reshape(n, 16, head_cols)], axis=1)
    (head_grad,), (grad_queries,) = order_after([head_grad], [grad_queries])
    head_grad = all_to_all(head_grad)
    gain_sum = head_grad[:, rows:].reshape(n, -1)[:, :gain_count].astype(F32)
    gain_sum = jnp.sum(gain_sum, axis=0).reshape(2, 3, rows)
    gain_sum = gain_sum[0] + gain_sum[1]
    head_grad = head_grad[:, :rows]
    out_sum, _ = scatter_small_rest("grad_output_w", out_pieces, n)
    (head_grad,), kv_pieces[1:2] = order_after([head_grad], kv_pieces[1:2])
    head_grad = rep_sum(head_grad)[::split]
    grad_output_proj = rep_join(out_sum.astype(BF16), 1).astype(F32)
    grad_queries = jnp.transpose(grad_queries[::split, :, : DN + DR], (1, 0, 2))
    grad_queries = grad_queries.reshape(both, reps, -1)
    grad_normed = sum(
        contract("tj,dj->td", grad_queries[:, i], whole_query[i]) for i in range(reps)
    )
    grad_first, _ = rms_backward(hidden, factor, attn_gain_f, grad_normed + grad_local)
    input_grads = (grad_first + grad_res).astype(BF16).reshape(MICRO, tok, width)

    grad_query_proj = jnp.transpose(head_grad[..., : DN + DR], (1, 0, 2)).reshape(rows, -1)
    grad_expand_proj = jnp.transpose(
        head_grad[..., DN + DR :].reshape(H, R // n, DN + DV), (1, 0, 2)
    ).reshape(R // n, H * (DN + DV))

    kv_blocks = jnp.concatenate(kv_pieces, axis=0)
    hidden_all, (grad_queries,) = order_after(hidden_all, [grad_queries])
    gain_cols = lax.dynamic_slice_in_dim(attn_gain_f, me * rows, rows, 0)
    hidden_cols = jnp.concatenate(
        [lax.dynamic_slice_in_dim(item, me * rows, rows, 2) for item in hidden_all], axis=0
    ).reshape(n, MICRO, tok, rows)
    factors = jnp.swapaxes(att[8].reshape(MICRO, n, tok, 1), 0, 1)
    normed_cols = (hidden_cols.astype(F32) * factors * gain_cols).astype(BF16)
    latent_total = contract(
        "tj,td->jd", kv_blocks.reshape(-1, R + DR), normed_cols.reshape(-1, rows)
    )
    latent_total = rep_sum(latent_total)
    grad_latent_proj = latent_total.T

    gain_sum = gain_sum + sum(rep_pull(gain_sum, reps, step) for step in range(1, reps))

    return (
        outputs,
        input_grads,
        gain_sum[0],
        grad_query_proj,
        grad_latent_proj,
        gain_sum[2, : R // n],
        grad_expand_proj,
        grad_output_proj,
        gain_sum[1],
        grad_shared_gate,
        grad_shared_lift,
        grad_shared_down,
        jnp.swapaxes(grad_expert_gate, 0, 1)[None],
        jnp.swapaxes(grad_expert_lift, 0, 1)[None],
        grad_expert_down[None],
    )


def solution(mesh):
    in_specs = (
        P("rep", "fsdp", None),
        P("rep", "fsdp", None),
        P("rep"),
        P("rep", "fsdp", None),
        P("rep", "fsdp", None),
        P("fsdp"),
        P("fsdp", None),
        P("fsdp", None),
        P("fsdp"),
        P("fsdp", None),
        P("fsdp", None),
        P("fsdp"),
        P("fsdp", None),
        P("fsdp", None),
        P("fsdp", None),
        P("fsdp", None, "rep"),
        P("fsdp", None, "rep"),
        P("fsdp", "rep", None),
    )
    out_specs = (
        P("rep", "fsdp", None),
        P("rep", "fsdp", None),
        P("fsdp"),
        P("fsdp", None),
        P("fsdp", None),
        P("fsdp"),
        P("fsdp", None),
        P("fsdp", None),
        P("fsdp"),
        P("fsdp", None),
        P("fsdp", None),
        P("fsdp", None),
        P("fsdp", None, "rep"),
        P("fsdp", None, "rep"),
        P("fsdp", "rep", None),
    )
    return jax.shard_map(body, mesh=mesh, in_specs=in_specs, out_specs=out_specs, check_vma=False)
```
